32 devices in a mesh: groups: 2 (over y), fsdp: 2 (over x), expert: 4 (over z), tensor: 2 (over core).
Axes of the slice: x: 2, y: 2, z: 4, core: 2. Of those that a mesh axis runs over, the one named last changes fastest.
Arguments:
- resid: bfloat16 [32, 6144], P(('groups', 'fsdp', 'expert', 'tensor')), parts along dimension 0, may hold values from -24 to 24
- query: bfloat16 [32, 6144], P(('groups', 'fsdp', 'expert', 'tensor')), parts along dimension 0, may hold values from -9 to 9
- cache: bfloat16 [2, 32, 64, 1024], P(None, ('groups', 'fsdp', 'expert', 'tensor')), parts along dimension 1, may hold values from -4 to 4
- new_key_value: bfloat16 [2, 32, 1024], P(None, ('groups', 'fsdp', 'expert', 'tensor')), parts along dimension 1, may hold values from -4 to 4
- lengths: int32 [32], P(('groups', 'fsdp', 'expert', 'tensor')), parts along dimension 0, may hold values from 2 to 64, as said below
- norm_gain: float32 [6144], replicated, may hold values from 0.1 to 1.9
- router_weight: bfloat16 [6144, 4], replicated, may hold values from -0.078125 to 0.078125
- choices: int32 [32, 2], P('groups'), parts along dimension 0, may hold values from 0 to 3, all different within a row; in each aligned block of 16 rows (0 to 15, 16 to 31, ...) at most 10 rows name the same one
- overflow: int32 [32], P('groups'), parts along dimension 0, may hold values 0 or 1
- up_weight: bfloat16 [4, 8192, 6144], P('expert', 'tensor', 'fsdp'), may hold values from -0.078125 to 0.078125
- down_weight: bfloat16 [4, 8192, 6144], P('expert', 'tensor', 'fsdp'), may hold values from -0.0625 to 0.0625
Outputs:
- stream: bfloat16 [32, 6144], P(('groups', 'fsdp', 'expert', 'tensor')), parts along dimension 0
- moe_out: bfloat16 [32, 6144], P(('groups', 'expert', 'tensor'), 'fsdp'), parts along dimension 0
The draws below stay inside these ranges and needn't reach their ends.
There are 2 independent parts, one for each index of `groups`. The reference program is written for one: setup_inputs(seed, part) draws one part's arguments, and reference() takes and returns one part's arrays. A program takes and returns all parts, laid end to end along the dimension named above; an argument that names none is the same for every part. Nothing has to cross between parts.
Inputs may be any that keep to these rules, and one draw needn't show every extreme that they name: `lengths`: at least one row uses all 64 cached positions. `choices`: each row names two different experts; no expert is named by more than 10 of the 16 rows, and one expert is named by exactly 10.
All inputs are finite; a program needn't handle non-finite values.
Results may differ from the reference program's by a relative error of at most 0.0075.
Values may be sent and summed in bfloat16 or wider, within the bound.
A program may use at most 256 MiB of HBM per device.

```python
import math
import jax
import jax.numpy as jnp
import numpy as np
from jax import lax

D = 6144
QUERY_HEADS = 48
KEY_VALUE_HEADS = 8
HEAD_SIZE = 128
HID = 8192
CACHE_POSITIONS = 64
EXP = 4
DECODE_ROWS = 16
CAP = 10


def draw_cache(key, part):
    key = jax.random.fold_in(key, 11)
    value_rows = jnp.clip(jax.random.normal(key, (2, DECODE_ROWS, CACHE_POSITIONS, KEY_VALUE_HEADS * HEAD_SIZE), jnp.float32), -4.0, 4.0)
    return value_rows.astype(jnp.bfloat16)


def draw_query(key, part):
    key = jax.random.fold_in(key, 12)
    value_rows = jnp.clip(jax.random.normal(key, (DECODE_ROWS, QUERY_HEADS * HEAD_SIZE), jnp.float32), -4.0, 4.0)
    return value_rows.astype(jnp.bfloat16)


def draw_resid(key, part):
    key = jax.random.fold_in(key, 13)
    key_rows, key_cols, key_base = jax.random.split(key, 3)
    row_scale = jnp.exp(jax.random.uniform(key_rows, (DECODE_ROWS, 1), jnp.float32, math.log(0.3), math.log(3.0)))
    col_scale = jnp.exp(jax.random.uniform(key_cols, (1, D), jnp.float32, math.log(0.3), math.log(3.0)))
    base = jax.random.normal(key_base, (DECODE_ROWS, D), jnp.float32)
    return jnp.clip(base * row_scale * col_scale, -24.0, 24.0).astype(jnp.bfloat16)


def draw_lengths(key, part):
    key = jax.random.fold_in(key, 14)
    key_drawn, key_spot = jax.random.split(key)
    drawn = jax.random.randint(key_drawn, (DECODE_ROWS,), 2, CACHE_POSITIONS + 1)
    spot = jax.random.randint(key_spot, (), 0, DECODE_ROWS)
    return jnp.where(jnp.arange(DECODE_ROWS) == spot, CACHE_POSITIONS, drawn).astype(jnp.int32)


def touch_ends(values, stream_key, low, high):
    dims = values.shape
    spot = [jax.random.randint(jax.random.fold_in(stream_key, axis), (), 0, dims[axis]) for axis in range(len(dims))]
    values = values.at[tuple(spot)].set(low)
    longest = dims.index(max(dims))
    spot[longest] = (spot[longest] + 1) % dims[longest]
    return values.at[tuple(spot)].set(high)


def block_levels(rng, extent, pieces, least, largest):
    loudness = 1.0
    for axis_at, parts in pieces:
        steps = jax.random.uniform(jax.random.fold_in(jax.random.fold_in(rng, 6), axis_at), (parts,), jnp.float32, least / len(pieces), largest / len(pieces))
        loudness = loudness * jnp.repeat(jnp.exp(steps), extent[axis_at] // parts).reshape((-1,) + (1,) * (len(extent) - 1 - axis_at))
    return loudness


def shared_out(own_key, own, number, rows, amount, top, most, skew):
    sequence = jax.random.permutation(own_key, amount)
    packed, usual = load_shares(amount, rows * top, most, skew, True), load_shares(amount, rows * top, most, skew, False)
    places = jnp.arange(amount)

    def named(tallies, turn):
        used = int((tallies > 0).sum())
        fixed = max(1, used // 4)
        passed = fixed + (places - fixed + turn * (used - fixed)) % max(1, amount - fixed)
        return jnp.zeros((amount,), jnp.int32).at[sequence[jnp.where(places < fixed, places, passed)]].set(jnp.asarray(tallies, jnp.int32))

    tallies = jnp.where(number % 4 == 0, named(packed, number // 4), named(usual, number - number // 4 - 1))
    mixed = jax.random.permutation(jax.random.fold_in(own, 3), amount)
    donor, sink = mixed[0:amount // 2 * 2:2], mixed[1:amount // 2 * 2:2]
    room = jnp.minimum(tallies[donor] - 1, most - tallies[sink]) // 2
    room = jnp.where((donor == sequence[0]) | (sink == sequence[0]) | (tallies[sink] == 0), 0, jnp.maximum(room, 0))
    passed = jax.random.randint(jax.random.fold_in(own, 4), (amount // 2,), 0, 1 << 20) % (room + 1)
    tallies = tallies.at[donor].add(-passed).at[sink].add(passed)
    items = jnp.searchsorted(jnp.cumsum(tallies), jnp.arange(rows * top), side="right").astype(jnp.int32)
    grid = items.reshape(top, rows).T
    grid = grid[jax.random.permutation(jax.random.fold_in(own, 1), rows)]
    turn = jax.random.randint(jax.random.fold_in(own, 2), (rows, 1), 0, top)
    return jnp.take_along_axis(grid, (jnp.arange(top)[None, :] + turn) % top, axis=1)


def load_shares(count, total, limit, slope, full):
    portions = [(1 << 20) // math.isqrt(rank ** slope) + 1 for rank in range(1, count + 1)]
    largest = limit if full else min(limit, max(-(-total // count), total * portions[0] // sum(portions)))
    least = 1 if total - largest >= count - 1 else 0
    holding, surplus = [largest] + [least] * (count - 1), total - largest - least * (count - 1)
    while surplus > 0:
        free = [i for i in range(1, count) if holding[i] < largest] or [i for i in range(1, count) if holding[i] < limit]
        whole, remaining = sum([portions[i] for i in free]), surplus
        for i in free:
            more = min(limit - holding[i], max(1, remaining * portions[i] // whole), surplus)
            holding[i] = holding[i] + more
            surplus = surplus - more
    return np.array(holding)


def scatter_about(key, shape, width, reach, cuts=(), held_as=jnp.bfloat16):
    factor_of = block_levels(key, shape, cuts, -0.22, 0.18) if cuts else 1.0
    values = jax.random.normal(key, shape, jnp.float32) * width * factor_of
    return jnp.minimum(jnp.maximum(values, -reach), reach).astype(held_as)


def setup_inputs(seed: int = 0, part: int = 0) -> dict:
    arg_keys = jax.random.split(jax.random.key(seed), 12)
    own_keys = jax.random.split(jax.random.fold_in(arg_keys[11], part), 12)
    resid = draw_resid(jax.random.fold_in(jax.random.fold_in(arg_keys[11], part), 71), part)
    query = draw_query(jax.random.fold_in(jax.random.fold_in(arg_keys[11], part), 71), part)
    cache = draw_cache(jax.random.fold_in(jax.random.fold_in(arg_keys[11], part), 71), part)
    new_key_value = scatter_about(own_keys[3], (2, DECODE_ROWS, KEY_VALUE_HEADS * HEAD_SIZE), 1.0, 4.0, ((1, 16),))
    lengths = draw_lengths(jax.random.fold_in(jax.random.fold_in(arg_keys[11], part), 71), part)
    norm_gain = jnp.clip(1.0 + 0.18 * jax.random.normal(arg_keys[5], (D,), jnp.float32), 0.1, 1.9)
    router_weight = scatter_about(arg_keys[6], (D, EXP), D ** -0.5, 0.078125)
    choices_keys = jax.random.split(jax.random.fold_in(own_keys[7], 1), DECODE_ROWS // DECODE_ROWS)
    choices_turns = jax.random.permutation(jax.random.fold_in(own_keys[7], 3), DECODE_ROWS // DECODE_ROWS)
    choices = jax.vmap(lambda own, number: shared_out(jax.random.fold_in(own_keys[7], 2), own, number, DECODE_ROWS, EXP, 2, CAP, 2))(choices_keys, choices_turns).reshape((DECODE_ROWS, 2))
    overflow = touch_ends((jax.random.randint(own_keys[8], (DECODE_ROWS,), 0, 4) < 1).astype(jnp.int32), jax.random.fold_in(own_keys[8], 1), 0, 1)
    up_weight = scatter_about(arg_keys[9], (EXP, HID, D), D ** -0.5, 0.078125, ((0, 4), (1, 2), (2, 2)))
    down_weight = scatter_about(arg_keys[10], (EXP, HID, D), HID ** -0.5, 0.0625, ((0, 4), (1, 2), (2, 2)))
    return dict(resid=resid, query=query, cache=cache, new_key_value=new_key_value, lengths=lengths, norm_gain=norm_gain, router_weight=router_weight, choices=choices, overflow=overflow, up_weight=up_weight, down_weight=down_weight)


def attend(query, cache, new_key_value, lengths):
    count_of_rows = query.shape[0]
    heads_per_group = QUERY_HEADS // KEY_VALUE_HEADS
    inv_root = 1.0 / math.sqrt(HEAD_SIZE)
    query_rows = query.astype(jnp.float32).reshape(count_of_rows, KEY_VALUE_HEADS, heads_per_group, HEAD_SIZE)
    resident_keys = cache[0].astype(jnp.float32).reshape(count_of_rows, CACHE_POSITIONS, KEY_VALUE_HEADS, HEAD_SIZE)
    resident_values = cache[1].astype(jnp.float32).reshape(count_of_rows, CACHE_POSITIONS, KEY_VALUE_HEADS, HEAD_SIZE)
    new_token_key = new_key_value[0].astype(jnp.float32).reshape(count_of_rows, KEY_VALUE_HEADS, HEAD_SIZE)
    new_token_value = new_key_value[1].astype(jnp.float32).reshape(count_of_rows, KEY_VALUE_HEADS, HEAD_SIZE)
    scores = jnp.einsum('rgqd,rlgd->rgql', query_rows, resident_keys) * inv_root
    own_score = jnp.einsum('rgqd,rgd->rgq', query_rows, new_token_key) * inv_root
    visible = jnp.arange(CACHE_POSITIONS)[None, :] < lengths[:, None]
    scores = jnp.where(visible[:, None, None, :], scores, -1e+30)
    highest = jnp.maximum(lax.optimization_barrier(jnp.max(scores, axis=-1)), own_score)
    raised = jnp.exp(scores - highest[..., None])
    raised_own = jnp.exp(own_score - highest)
    normalizer = lax.optimization_barrier(jnp.sum(raised, axis=-1)) + raised_own
    attn_prob = (raised / normalizer[..., None]).astype(jnp.bfloat16)
    prob_own = (raised_own / normalizer).astype(jnp.bfloat16)
    attended = jnp.einsum('rgql,rlgd->rgqd', attn_prob.astype(jnp.float32), resident_values)
    attended = attended + prob_own.astype(jnp.float32)[..., None] * new_token_value[:, :, None, :]
    return attended.reshape(count_of_rows, QUERY_HEADS * HEAD_SIZE)

def routing(normed, router_weight, choices, overflow):
    logits = jnp.dot(normed, router_weight, preferred_element_type=jnp.float32)
    labels = jnp.arange(router_weight.shape[1])
    first_pick = (choices[:, 0:1] == labels[None, :]).astype(jnp.float32)
    second = (choices[:, 1:2] == labels[None, :]).astype(jnp.float32)
    first_logit = lax.optimization_barrier(jnp.sum(logits * first_pick, axis=-1))
    second_logit = lax.optimization_barrier(jnp.sum(logits * second, axis=-1))
    first_prob = 1.0 / (1.0 + jnp.exp(second_logit - first_logit))
    kept_share = first_prob * (1.0 - overflow.astype(jnp.float32))
    return kept_share[:, None] * first_pick + (1.0 - kept_share)[:, None] * second

def reference(resid, query, cache, new_key_value, lengths, norm_gain, router_weight, choices, overflow, up_weight, down_weight):
    attended = attend(query, cache, new_key_value, lengths)
    stream = (resid.astype(jnp.float32) + attended).astype(jnp.bfloat16)
    levels = stream.astype(jnp.float32)
    normed = (levels * lax.rsqrt(lax.optimization_barrier(jnp.mean(levels * levels, axis=-1, keepdims=True)) + 1e-05) * norm_gain).astype(jnp.bfloat16)
    gate = routing(normed, router_weight, choices, overflow)

    def add_expert(running, inputs):
        up_mat, down_mat, gate_col = inputs
        pre_active = lax.dot_general(normed, up_mat, (((1,), (1,)), ((), ())), preferred_element_type=jnp.float32)
        active = jax.nn.silu(pre_active).astype(jnp.bfloat16)
        output = jnp.dot(active, down_mat, preferred_element_type=jnp.float32)
        return (running + gate_col[:, None] * output, None)
    combined, unused = lax.scan(add_expert, jnp.zeros((DECODE_ROWS, D), jnp.float32), (up_weight, down_weight, gate.T))
    return (stream, combined.astype(jnp.bfloat16))
```

```python
import math

import jax
import jax.numpy as jnp
from jax import lax
from jax.sharding import PartitionSpec as P

QUERY_HEADS = 48
KEY_VALUE_HEADS = 8
HEAD_SIZE = 128
CACHE_POSITIONS = 64


def attend(query, cache, new_key_value, lengths):
    count_of_rows = query.shape[0]
    heads_per_group = QUERY_HEADS // KEY_VALUE_HEADS
    inv_root = 1.0 / math.sqrt(HEAD_SIZE)
    query_rows = query.reshape(count_of_rows, KEY_VALUE_HEADS, heads_per_group, HEAD_SIZE)
    resident_keys = cache[0].reshape(count_of_rows, CACHE_POSITIONS, KEY_VALUE_HEADS, HEAD_SIZE)
    resident_values = cache[1].reshape(count_of_rows, CACHE_POSITIONS, KEY_VALUE_HEADS, HEAD_SIZE)
    new_token_key = new_key_value[0].reshape(count_of_rows, KEY_VALUE_HEADS, HEAD_SIZE)
    new_token_value = new_key_value[1].reshape(count_of_rows, KEY_VALUE_HEADS, HEAD_SIZE)
    scores = (
        jnp.einsum("rgqd,rlgd->rgql", query_rows, resident_keys, preferred_element_type=jnp.float32)
        * inv_root
    )
    own_score = (
        jnp.einsum("rgqd,rgd->rgq", query_rows, new_token_key, preferred_element_type=jnp.float32)
        * inv_root
    )
    visible = jnp.arange(CACHE_POSITIONS)[None, :] < lengths[:, None]
    scores = jnp.where(visible[:, None, None, :], scores, -1e30)
    highest = jnp.maximum(jnp.max(scores, axis=-1), own_score)
    raised = jnp.exp(scores - highest[..., None])
    raised_own = jnp.exp(own_score - highest)
    normalizer = jnp.sum(raised, axis=-1) + raised_own
    attn_prob = (raised / normalizer[..., None]).astype(jnp.bfloat16)
    prob_own = (raised_own / normalizer).astype(jnp.bfloat16)
    attended = jnp.einsum(
        "rgql,rlgd->rgqd", attn_prob, resident_values, preferred_element_type=jnp.float32
    )
    attended = (
        attended
        + prob_own.astype(jnp.float32)[..., None]
        * new_token_value.astype(jnp.float32)[:, :, None, :]
    )
    return attended.reshape(count_of_rows, QUERY_HEADS * HEAD_SIZE)


def expert_gate(every_row, router_weight, choices, overflow, my_expert):
    logits = jnp.dot(every_row, router_weight, preferred_element_type=jnp.float32)
    labels = jnp.arange(router_weight.shape[1])
    first_pick = (choices[:, 0:1] == labels[None, :]).astype(jnp.float32)
    second = (choices[:, 1:2] == labels[None, :]).astype(jnp.float32)
    first_logit = jnp.sum(logits * first_pick, axis=-1)
    second_logit = jnp.sum(logits * second, axis=-1)
    first_prob = 1.0 / (1.0 + jnp.exp(second_logit - first_logit))
    kept_share = first_prob * (1.0 - overflow.astype(jnp.float32))
    own_mask = (labels == my_expert).astype(jnp.float32)[None, :]
    return kept_share * jnp.sum(first_pick * own_mask, axis=-1) + (1.0 - kept_share) * jnp.sum(
        second * own_mask, axis=-1
    )


def shards(
    resid,
    query,
    cache,
    new_key_value,
    lengths,
    norm_gain,
    router_weight,
    choices,
    overflow,
    up_weight,
    down_weight,
):
    attended = attend(query, cache, new_key_value, lengths)
    stream = (resid.astype(jnp.float32) + attended).astype(jnp.bfloat16)
    levels = stream.astype(jnp.float32)
    normed = (
        levels * lax.rsqrt(jnp.mean(levels * levels, axis=-1, keepdims=True) + 1e-05) * norm_gain
    ).astype(jnp.bfloat16)
    every_row = lax.all_gather(normed, ("fsdp", "expert", "tensor"), axis=0, tiled=True)
    my_expert = lax.axis_index("expert")
    gate_mine = expert_gate(every_row, router_weight, choices, overflow, my_expert)
    features = up_weight.shape[2]
    my_features = lax.dynamic_slice_in_dim(
        every_row, lax.axis_index("fsdp") * features, features, axis=1
    )
    partial_active = lax.dot_general(
        my_features, up_weight[0], (((1,), (1,)), ((), ())), preferred_element_type=jnp.float32
    )
    pre_active = lax.psum_scatter(partial_active, "fsdp", scatter_dimension=1, tiled=True)
    active = jax.nn.silu(pre_active).astype(jnp.bfloat16)
    partial_value = jnp.dot(
        lax.all_gather(active, "fsdp", axis=1, tiled=True),
        down_weight[0],
        preferred_element_type=jnp.float32,
    )
    weighted = gate_mine[:, None] * partial_value
    combined = lax.psum_scatter(weighted, ("expert", "tensor"), scatter_dimension=0, tiled=True)
    return (stream, combined.astype(jnp.bfloat16))


def solution(mesh):
    return jax.shard_map(
        shards,
        mesh=mesh,
        in_specs=(
            P(("groups", "fsdp", "expert", "tensor"), None),
            P(("groups", "fsdp", "expert", "tensor"), None),
            P(None, ("groups", "fsdp", "expert", "tensor"), None, None),
            P(None, ("groups", "fsdp", "expert", "tensor"), None),
            P(("groups", "fsdp", "expert", "tensor")),
            P(),
            P(),
            P("groups", None),
            P("groups"),
            P("expert", "tensor", "fsdp"),
            P("expert", "tensor", "fsdp"),
        ),
        out_specs=(
            P(("groups", "fsdp", "expert", "tensor"), None),
            P(("groups", "expert", "tensor"), "fsdp"),
        ),
        check_vma=False,
    )
```

```python
import math

import jax
import jax.numpy as jnp
from jax import lax
from jax.experimental import pallas as pl
from jax.experimental.pallas import tpu as pltpu
from jax.sharding import PartitionSpec as P

QUERY_HEADS = 48
KEY_VALUE_HEADS = 8
HEAD_SIZE = 128
CACHE_POSITIONS = 64


def attend(query, cache, new_key_value, lengths):
    count_of_rows = query.shape[0]
    heads_per_group = QUERY_HEADS // KEY_VALUE_HEADS
    inv_root = 1.0 / math.sqrt(HEAD_SIZE)
    query_rows = query.reshape(count_of_rows, KEY_VALUE_HEADS, heads_per_group, HEAD_SIZE)
    resident_keys = cache[0].reshape(count_of_rows, CACHE_POSITIONS, KEY_VALUE_HEADS, HEAD_SIZE)
    resident_values = cache[1].reshape(count_of_rows, CACHE_POSITIONS, KEY_VALUE_HEADS, HEAD_SIZE)
    new_token_key = new_key_value[0].reshape(count_of_rows, KEY_VALUE_HEADS, HEAD_SIZE)
    new_token_value = new_key_value[1].reshape(count_of_rows, KEY_VALUE_HEADS, HEAD_SIZE)
    scores = (
        jnp.einsum("rgqd,rlgd->rgql", query_rows, resident_keys, preferred_element_type=jnp.float32)
        * inv_root
    )
    own_score = (
        jnp.einsum("rgqd,rgd->rgq", query_rows, new_token_key, preferred_element_type=jnp.float32)
        * inv_root
    )
    visible = jnp.arange(CACHE_POSITIONS)[None, :] < lengths[:, None]
    scores = jnp.where(visible[:, None, None, :], scores, -1e30)
    highest = jnp.maximum(jnp.max(scores, axis=-1), own_score)
    raised = jnp.exp(scores - highest[..., None])
    raised_own = jnp.exp(own_score - highest)
    normalizer = jnp.sum(raised, axis=-1) + raised_own
    attn_prob = (raised / normalizer[..., None]).astype(jnp.bfloat16)
    prob_own = (raised_own / normalizer).astype(jnp.bfloat16)
    attended = jnp.einsum(
        "rgql,rlgd->rgqd", attn_prob, resident_values, preferred_element_type=jnp.float32
    )
    attended = (
        attended
        + prob_own.astype(jnp.float32)[..., None]
        * new_token_value.astype(jnp.float32)[:, :, None, :]
    )
    return attended.reshape(count_of_rows, QUERY_HEADS * HEAD_SIZE)


def expert_gate(every_row, router_weight, choices, overflow, my_expert):
    logits = jnp.dot(every_row, router_weight, preferred_element_type=jnp.float32)
    labels = jnp.arange(router_weight.shape[1])
    first_pick = (choices[:, 0:1] == labels[None, :]).astype(jnp.float32)
    second = (choices[:, 1:2] == labels[None, :]).astype(jnp.float32)
    first_logit = jnp.sum(logits * first_pick, axis=-1)
    second_logit = jnp.sum(logits * second, axis=-1)
    first_prob = 1.0 / (1.0 + jnp.exp(second_logit - first_logit))
    kept_share = first_prob * (1.0 - overflow.astype(jnp.float32))
    own_mask = (labels == my_expert).astype(jnp.float32)[None, :]
    return kept_share * jnp.sum(first_pick * own_mask, axis=-1) + (1.0 - kept_share) * jnp.sum(
        second * own_mask, axis=-1
    )


def shards(
    resid,
    query,
    cache,
    new_key_value,
    lengths,
    norm_gain,
    router_weight,
    choices,
    overflow,
    up_weight,
    down_weight,
):
    attended = attend(query, cache, new_key_value, lengths)
    stream = (resid.astype(jnp.float32) + attended).astype(jnp.bfloat16)
    levels = stream.astype(jnp.float32)
    normed = (
        levels * lax.rsqrt(jnp.mean(levels * levels, axis=-1, keepdims=True) + 1e-05) * norm_gain
    ).astype(jnp.bfloat16)
    every_row = lax.all_gather(normed, ("fsdp", "expert", "tensor"), axis=0, tiled=True)
    my_expert = lax.axis_index("expert")
    gate_mine = expert_gate(every_row, router_weight, choices, overflow, my_expert)
    features = up_weight.shape[2]
    my_features = lax.dynamic_slice_in_dim(
        every_row, lax.axis_index("fsdp") * features, features, axis=1
    )
    partial_active = lax.dot_general(
        my_features, up_weight[0], (((1,), (1,)), ((), ())), preferred_element_type=jnp.float32
    )
    pre_active = lax.psum_scatter(partial_active, "fsdp", scatter_dimension=1, tiled=True)
    active = jax.nn.silu(pre_active).astype(jnp.bfloat16)
    partial_value = jnp.dot(
        lax.all_gather(active, "fsdp", axis=1, tiled=True),
        down_weight[0],
        preferred_element_type=jnp.float32,
    )
    weighted = gate_mine[:, None] * partial_value
    combined = lax.psum_scatter(weighted, ("expert", "tensor"), scatter_dimension=0, tiled=True)
    return (stream, combined.astype(jnp.bfloat16))


MESH = pl.DeviceIdType.MESH
GROUPS, FSDP, EXPERTS, CORES = 2, 2, 4, 2
PLANE = FSDP * EXPERTS
BLOCKS = GROUPS * CORES
ROWS = BLOCKS * PLANE
UP_CHUNKS = 4
OUT_CHUNKS = 3


def place_of(slot):
    block, inner = divmod(slot, PLANE)
    group, core = divmod(block, CORES)
    row = inner * CORES + core
    expert_to, rest = divmod(row, 4)
    core_to, pair = divmod(rest, 2)
    return group * 16 + core_to * 8 + expert_to * 2 + pair


def layer_kernel(
    lengths,
    choices,
    overflow,
    resid,
    query,
    new_kv,
    gain,
    cache,
    router,
    up,
    down,
    stream_out,
    moe_out,
    kv,
    rt,
    upw,
    downw,
    qbd,
    r48,
    payload,
    rows_in,
    rows_all,
    xs,
    x,
    meta,
    logit_mine,
    logit_in,
    pre_mine,
    pre_send,
    pre_in,
    act,
    acc,
    own_out,
    a_send,
    a_in,
    z_send,
    z_in,
    local_sem,
    up_sem,
    down_sem,
    row_send_sem,
    row_recv_sem,
    block_send_sem,
    block_recv_sem,
    pair_send_sem,
    pair_recv_sem,
    pre_send_sem,
    pre_recv_sem,
    a_send_sem,
    a_recv_sem,
    z_send_sem,
    z_recv_sem,
):
    g = lax.axis_index("groups")
    f = lax.axis_index("fsdp")
    e = lax.axis_index("expert")
    t = lax.axis_index("tensor")
    here = f * EXPERTS + e
    block = g * CORES + t
    features = x.shape[1]
    pieces = features // HEAD_SIZE
    heads = 2 * pieces
    group_heads = heads // KEY_VALUE_HEADS
    hidden = upw.shape[1]
    width = moe_out.shape[1] // OUT_CHUNKS
    half = width // 2

    def remote(src, dst, send, recv, device):
        return pltpu.make_async_remote_copy(
            src_ref=src,
            dst_ref=dst,
            send_sem=send,
            recv_sem=recv,
            device_id=device,
            device_id_type=MESH,
        )

    def plane_peer(k):
        other = lax.rem(here + k, PLANE)
        return other // EXPERTS, lax.rem(other, EXPERTS)

    def block_peer(k):
        other = lax.rem(block + k, BLOCKS)
        return other, other // CORES, lax.rem(other, CORES)

    key_copy = pltpu.make_async_copy(cache.at[0, 0], kv.at[0], local_sem.at[0])
    value_copy = pltpu.make_async_copy(cache.at[1, 0], kv.at[1], local_sem.at[1])
    key_copy.start()
    value_copy.start()

    barrier = pltpu.get_barrier_semaphore()
    for k in range(1, PLANE):
        f2, e2 = plane_peer(k)
        pl.semaphore_signal(barrier, inc=1, device_id=(g, f2, e2, t), device_id_type=MESH)
    for k in range(1, BLOCKS):
        _, g2, t2 = block_peer(k)
        pl.semaphore_signal(barrier, inc=1, device_id=(g2, f, e, t2), device_id_type=MESH)

    router_copy = pltpu.make_async_copy(
        router.at[pl.ds(pl.multiple_of(f * features, features), features), :], rt, local_sem.at[2]
    )

    def up_copy(c):
        start = pl.multiple_of(g * (UP_CHUNKS * hidden) + c * hidden, hidden)
        return pltpu.make_async_copy(up.at[0, pl.ds(start, hidden), :], upw.at[c], up_sem.at[c])

    def down_copy(c):
        start = pl.multiple_of(g * (UP_CHUNKS * hidden) + c * hidden, hidden)
        return pltpu.make_async_copy(
            down.at[0, pl.ds(start, hidden), :],
            downw.at[pl.ds(c * hidden, hidden), :],
            down_sem.at[c],
        )

    router_copy.start()
    for c in range(UP_CHUNKS):
        up_copy(c).start()
    for c in range(UP_CHUNKS):
        down_copy(c).start()

    qbd[...] = jnp.zeros_like(qbd)
    query_row = query[...].astype(jnp.float32)
    resid_row = resid[...].astype(jnp.float32)
    for h in range(heads):
        kv_at = h // group_heads * HEAD_SIZE
        qbd[h : h + 1, kv_at : kv_at + HEAD_SIZE] = query_row[:, h * HEAD_SIZE : (h + 1) * HEAD_SIZE]
        r48[h : h + 1, :] = resid_row[:, h * HEAD_SIZE : (h + 1) * HEAD_SIZE]
    inv_root = 1.0 / math.sqrt(HEAD_SIZE)
    new_key = new_kv[0].astype(jnp.float32)
    new_value = new_kv[1].astype(jnp.float32)
    spread = qbd[...]
    own_score = jnp.sum(spread * new_key, axis=-1, keepdims=True) * inv_root
    spread = spread.astype(jnp.bfloat16)
    key_copy.wait()
    scores = (
        lax.dot_general(
            spread, kv[0], (((1,), (1,)), ((), ())), preferred_element_type=jnp.float32
        )
        * inv_root
    )
    position = lax.broadcasted_iota(jnp.int32, scores.shape, 1)
    scores = jnp.where(position < lengths[0], scores, -1e30)
    highest = jnp.maximum(jnp.max(scores, axis=-1, keepdims=True), own_score)
    raised = jnp.exp(scores - highest)
    raised_own = jnp.exp(own_score - highest)
    normalizer = jnp.sum(raised, axis=-1, keepdims=True) + raised_own
    attn_prob = (raised / normalizer).astype(jnp.bfloat16)
    prob_own = (raised_own / normalizer).astype(jnp.bfloat16).astype(jnp.float32)
    value_copy.wait()
    mixed = jnp.dot(attn_prob, kv[1], preferred_element_type=jnp.float32) + prob_own * new_value
    head_at = lax.broadcasted_iota(jnp.int32, (heads, HEAD_SIZE), 0)
    attended = mixed[:, :HEAD_SIZE]
    for group in range(1, KEY_VALUE_HEADS):
        attended = jnp.where(
            head_at >= group * group_heads,
            mixed[:, group * HEAD_SIZE : (group + 1) * HEAD_SIZE],
            attended,
        )
    levels = (r48[...] + attended).astype(jnp.bfloat16).astype(jnp.float32)
    total = jnp.sum(jnp.sum(levels * levels, axis=1, keepdims=True), axis=0, keepdims=True)
    normed = levels * lax.rsqrt(total / (heads * HEAD_SIZE) + 1e-05) * gain[...]
    filler = jnp.zeros((payload.shape[1] - pieces, HEAD_SIZE), jnp.float32)
    for part in range(FSDP):
        payload[part] = jnp.concatenate(
            [normed[part * pieces : (part + 1) * pieces], filler], axis=0
        ).astype(jnp.bfloat16)

    pl.semaphore_wait(barrier, PLANE - 1 + BLOCKS - 1)

    row_copies = []
    for k in range(1, PLANE):
        f2, e2 = plane_peer(k)
        row_copies.append(
            remote(
                payload.at[f2],
                rows_in.at[here],
                row_send_sem.at[k - 1],
                row_recv_sem.at[k - 1],
                (g, f2, e2, t),
            )
        )
        row_copies[-1].start()
    rows_in[here] = payload[f]

    for h in range(heads):
        stream_out[:, h * HEAD_SIZE : (h + 1) * HEAD_SIZE] = levels[h : h + 1].astype(jnp.bfloat16)

    at = lax.broadcasted_iota(jnp.int32, (16, HEAD_SIZE), 0)
    lane = lax.broadcasted_iota(jnp.int32, (16, HEAD_SIZE), 1)
    facts = jnp.zeros((16, HEAD_SIZE), jnp.float32)
    for row in range(16):
        place = row % 4 // 2 * 8 + row // 4 * 2 + row % 2
        for col, value in enumerate((choices[row, 0], choices[row, 1], overflow[row])):
            facts = jnp.where((at == place) & (lane == col), value.astype(jnp.float32), facts)
    meta[g] = facts
    meta_copy = remote(
        meta.at[g], meta.at[g], pair_send_sem.at[0], pair_recv_sem.at[0], (1 - g, f, e, t)
    )
    meta_copy.start()

    for copy in row_copies:
        copy.wait_recv()
    mine = rows_in[...].astype(jnp.float32)[:, :pieces]
    rows_all[block] = mine.reshape(PLANE * pieces, HEAD_SIZE).astype(jnp.bfloat16)
    block_copies = []
    for k in range(1, BLOCKS):
        _, g2, t2 = block_peer(k)
        block_copies.append(
            remote(
                rows_all.at[block],
                rows_all.at[block],
                block_send_sem.at[k - 1],
                block_recv_sem.at[k - 1],
                (g2, f, e, t2),
            )
        )
        block_copies[-1].start()
    for copy in block_copies:
        copy.wait_recv()

    for b in range(BLOCKS):
        taken = rows_all[b].astype(jnp.float32)
        for i in range(PLANE):
            to = place_of(b * PLANE + i) * pieces
            xs[to : to + pieces, :] = taken[i * pieces : (i + 1) * pieces]
    for j in range(pieces):
        x[:, j * HEAD_SIZE : (j + 1) * HEAD_SIZE] = xs[pl.ds(j, ROWS, stride=pieces), :].astype(
            jnp.bfloat16
        )

    across = (g, 1 - f, e, t)
    router_copy.wait()
    labels = rt.shape[1]
    logit_mine[...] = jnp.zeros_like(logit_mine)
    logit_mine[:, :labels] = jnp.dot(x[...], rt[...], preferred_element_type=jnp.float32)
    logit_copy = remote(logit_mine, logit_in, pair_send_sem.at[1], pair_recv_sem.at[1], across)
    logit_copy.start()

    def pre_copy(c):
        return remote(
            pre_send.at[c], pre_in.at[c], pre_send_sem.at[c], pre_recv_sem.at[c], across
        )

    def up_step(c, carry):
        up_copy(c).wait()
        partial = lax.dot_general(
            x[...], upw[c], (((1,), (1,)), ((), ())), preferred_element_type=jnp.float32
        )
        pre_mine[c] = partial
        pre_send[c] = partial.astype(jnp.bfloat16)
        pre_copy(c).start()
        return carry

    lax.fori_loop(0, UP_CHUNKS, up_step, 0)

    meta_copy.wait_recv()
    logit_copy.wait_recv()
    logits = logit_mine[...] + logit_in[...]
    named = jnp.concatenate([meta[0], meta[1]], axis=0)
    label = lax.broadcasted_iota(jnp.int32, logits.shape, 1).astype(jnp.float32)
    first, second, full = named[:, 0:1], named[:, 1:2], named[:, 2:3]
    first_logit = jnp.sum(jnp.where(label == first, logits, 0.0), axis=1, keepdims=True)
    second_logit = jnp.sum(jnp.where(label == second, logits, 0.0), axis=1, keepdims=True)
    first_prob = 1.0 / (1.0 + jnp.exp(second_logit - first_logit))
    kept = first_prob * (1.0 - full)
    my_label = e.astype(jnp.float32)
    gate = jnp.where(first == my_label, kept, 0.0) + jnp.where(second == my_label, 1.0 - kept, 0.0)

    for c in range(UP_CHUNKS):
        down_copy(c).wait()

    def activate(c):
        pre_copy(c).wait_recv()
        value = pre_mine[c] + pre_in[c].astype(jnp.float32)
        act[:, c * hidden : (c + 1) * hidden] = (value / (1.0 + jnp.exp(-value))).astype(
            jnp.bfloat16
        )

    split = UP_CHUNKS // 2 * hidden
    for c in range(UP_CHUNKS // 2):
        activate(c)
    for n in range(OUT_CHUNKS):
        cols = slice(n * width, (n + 1) * width)
        acc[:, cols] = jnp.dot(
            act[:, :split], downw[:split, cols], preferred_element_type=jnp.float32
        )
    for c in range(UP_CHUNKS // 2, UP_CHUNKS):
        activate(c)

    a_copies = [[] for _ in range(OUT_CHUNKS)]
    z_copies = [[] for _ in range(OUT_CHUNKS)]

    def multiply(n):
        cols = slice(n * width, (n + 1) * width)
        value = gate * (
            acc[:, cols]
            + jnp.dot(act[:, split:], downw[split:, cols], preferred_element_type=jnp.float32)
        )
        for b in range(BLOCKS):
            rows = value[b * PLANE : (b + 1) * PLANE]
            folded = jnp.concatenate([rows[:, :half], rows[:, half:]], axis=0)
            own_out[b] = folded
            a_send[n, b] = folded.astype(jnp.bfloat16)
        acc[0:16, n * width : n * width + half] = own_out[block]
        for k in range(1, BLOCKS):
            b2, g2, t2 = block_peer(k)
            at_sem = n * (BLOCKS - 1) + k - 1
            a_copies[n].append(
                remote(
                    a_send.at[n, b2],
                    a_in.at[n, k - 1],
                    a_send_sem.at[at_sem],
                    a_recv_sem.at[at_sem],
                    (g2, f, e, t2),
                )
            )
            a_copies[n][-1].start()

    def add_blocks(n):
        value = acc[0:16, n * width : n * width + half]
        for k in range(1, BLOCKS):
            a_copies[n][k - 1].wait_recv()
            value = value + a_in[n, k - 1].astype(jnp.float32)
        for to in range(EXPERTS):
            z_send[n, to, :, :half] = value[2 * to : 2 * to + 2]
            z_send[n, to, :, half:] = value[PLANE + 2 * to : PLANE + 2 * to + 2]
        for k in range(1, EXPERTS):
            e2 = lax.rem(e + k, EXPERTS)
            at_sem = n * (EXPERTS - 1) + k - 1
            z_copies[n].append(
                remote(
                    z_send.at[n, e2],
                    z_in.at[n, k - 1],
                    z_send_sem.at[at_sem],
                    z_recv_sem.at[at_sem],
                    (g, f, e2, t),
                )
            )
            z_copies[n][-1].start()

    for n in range(OUT_CHUNKS):
        multiply(n)
        if n > 0:
            add_blocks(n - 1)
    add_blocks(OUT_CHUNKS - 1)
    for n in range(OUT_CHUNKS):
        value = z_send[n, e]
        for k in range(1, EXPERTS):
            z_copies[n][k - 1].wait_recv()
            value = value + z_in[n, k - 1]
        moe_out[:, n * width : (n + 1) * width] = value.astype(jnp.bfloat16)

    for copy in row_copies + block_copies + [meta_copy, logit_copy]:
        copy.wait_send()
    for c in range(UP_CHUNKS):
        pre_copy(c).wait_send()
    for n in range(OUT_CHUNKS):
        for copy in a_copies[n] + z_copies[n]:
            copy.wait_send()


def kernel_shards(
    resid,
    query,
    cache,
    new_key_value,
    lengths,
    norm_gain,
    router_weight,
    choices,
    overflow,
    up_weight,
    down_weight,
):
    _, hidden_all, features = up_weight.shape
    hidden = hidden_all // GROUPS
    chunk = hidden // UP_CHUNKS
    width = features // OUT_CHUNKS
    pieces = features // HEAD_SIZE
    padded = -(-pieces // 16) * 16
    heads = FSDP * pieces
    kv_features = cache.shape[3]
    f32, bf16 = jnp.float32, jnp.bfloat16
    vmem = pl.BlockSpec(memory_space=pltpu.VMEM)
    smem = pl.BlockSpec(memory_space=pltpu.SMEM)
    anywhere = pl.BlockSpec(memory_space=pl.ANY)
    dma = pltpu.SemaphoreType.DMA
    return pl.pallas_call(
        layer_kernel,
        out_shape=(
            jax.ShapeDtypeStruct(resid.shape, bf16),
            jax.ShapeDtypeStruct((ROWS // (BLOCKS * EXPERTS), features), bf16),
        ),
        in_specs=[smem] * 3 + [vmem] * 4 + [anywhere] * 4,
        out_specs=(vmem, vmem),
        scratch_shapes=[
            pltpu.VMEM((2, CACHE_POSITIONS, kv_features), bf16),
            pltpu.VMEM((features, router_weight.shape[1]), bf16),
            pltpu.VMEM((UP_CHUNKS, chunk, features), bf16),
            pltpu.VMEM((hidden, features), bf16),
            pltpu.VMEM((heads, kv_features), f32),
            pltpu.VMEM((heads, HEAD_SIZE), f32),
            pltpu.VMEM((FSDP, padded, HEAD_SIZE), bf16),
            pltpu.VMEM((PLANE, padded, HEAD_SIZE), bf16),
            pltpu.VMEM((BLOCKS, PLANE * pieces, HEAD_SIZE), bf16),
            pltpu.VMEM((ROWS * pieces, HEAD_SIZE), f32),
            pltpu.VMEM((ROWS, features), bf16),
            pltpu.VMEM((GROUPS, 16, HEAD_SIZE), f32),
            pltpu.VMEM((ROWS, HEAD_SIZE), f32),
            pltpu.VMEM((ROWS, HEAD_SIZE), f32),
            pltpu.VMEM((UP_CHUNKS, ROWS, chunk), f32),
            pltpu.VMEM((UP_CHUNKS, ROWS, chunk), bf16),
            pltpu.VMEM((UP_CHUNKS, ROWS, chunk), bf16),
            pltpu.VMEM((ROWS, hidden), bf16),
            pltpu.VMEM((ROWS, features), f32),
            pltpu.VMEM((BLOCKS, 16, width // 2), f32),
            pltpu.VMEM((OUT_CHUNKS, BLOCKS, 16, width // 2), bf16),
            pltpu.VMEM((OUT_CHUNKS, BLOCKS - 1, 16, width // 2), bf16),
            pltpu.VMEM((OUT_CHUNKS, EXPERTS, 2, width), f32),
            pltpu.VMEM((OUT_CHUNKS, EXPERTS - 1, 2, width), f32),
            dma((3,)),
            dma((UP_CHUNKS,)),
            dma((UP_CHUNKS,)),
            dma((PLANE - 1,)),
            dma((PLANE - 1,)),
            dma((BLOCKS - 1,)),
            dma((BLOCKS - 1,)),
            dma((2,)),
            dma((2,)),
            dma((UP_CHUNKS,)),
            dma((UP_CHUNKS,)),
            dma((OUT_CHUNKS * (BLOCKS - 1),)),
            dma((OUT_CHUNKS * (BLOCKS - 1),)),
            dma((OUT_CHUNKS * (EXPERTS - 1),)),
            dma((OUT_CHUNKS * (EXPERTS - 1),)),
        ],
        compiler_params=pltpu.CompilerParams(
            collective_id=0, has_side_effects=True, vmem_limit_bytes=48 * 1024 * 1024
        ),
        cost_estimate=pl.CostEstimate(
            flops=4 * ROWS * hidden * features,
            bytes_accessed=4 * hidden * features,
            transcendentals=ROWS * hidden,
        ),
        name="layer",
    )(
        lengths,
        choices,
        overflow,
        resid,
        query,
        new_key_value,
        norm_gain.reshape(heads, HEAD_SIZE),
        cache,
        router_weight,
        up_weight,
        down_weight,
    )


def solution(mesh):
    sizes = tuple(mesh.shape[name] for name in ("groups", "fsdp", "expert", "tensor"))
    in_kernel = sizes == (GROUPS, FSDP, EXPERTS, CORES)
    return jax.shard_map(
        kernel_shards if in_kernel else shards,
        mesh=mesh,
        in_specs=(
            P(("groups", "fsdp", "expert", "tensor"), None),
            P(("groups", "fsdp", "expert", "tensor"), None),
            P(None, ("groups", "fsdp", "expert", "tensor"), None, None),
            P(None, ("groups", "fsdp", "expert", "tensor"), None),
            P(("groups", "fsdp", "expert", "tensor")),
            P(),
            P(),
            P("groups", None),
            P("groups"),
            P("expert", "tensor", "fsdp"),
            P("expert", "tensor", "fsdp"),
        ),
        out_specs=(
            P(("groups", "fsdp", "expert", "tensor"), None),
            P(("groups", "expert", "tensor"), "fsdp"),
        ),
        check_vma=False,
    )
```

```python
import math

import jax
import jax.numpy as jnp
from jax import lax
from jax.experimental import pallas as pl
from jax.experimental.pallas import tpu as pltpu
from jax.sharding import PartitionSpec as P

QUERY_HEADS = 48
KEY_VALUE_HEADS = 8
HEAD_SIZE = 128
CACHE_POSITIONS = 64


def attend(query, cache, new_key_value, lengths):
    count_of_rows = query.shape[0]
    heads_per_group = QUERY_HEADS // KEY_VALUE_HEADS
    inv_root = 1.0 / math.sqrt(HEAD_SIZE)
    query_rows = query.reshape(count_of_rows, KEY_VALUE_HEADS, heads_per_group, HEAD_SIZE)
    resident_keys = cache[0].reshape(count_of_rows, CACHE_POSITIONS, KEY_VALUE_HEADS, HEAD_SIZE)
    resident_values = cache[1].reshape(count_of_rows, CACHE_POSITIONS, KEY_VALUE_HEADS, HEAD_SIZE)
    new_token_key = new_key_value[0].reshape(count_of_rows, KEY_VALUE_HEADS, HEAD_SIZE)
    new_token_value = new_key_value[1].reshape(count_of_rows, KEY_VALUE_HEADS, HEAD_SIZE)
    scores = (
        jnp.einsum("rgqd,rlgd->rgql", query_rows, resident_keys, preferred_element_type=jnp.float32)
        * inv_root
    )
    own_score = (
        jnp.einsum("rgqd,rgd->rgq", query_rows, new_token_key, preferred_element_type=jnp.float32)
        * inv_root
    )
    visible = jnp.arange(CACHE_POSITIONS)[None, :] < lengths[:, None]
    scores = jnp.where(visible[:, None, None, :], scores, -1e30)
    highest = jnp.maximum(jnp.max(scores, axis=-1), own_score)
    raised = jnp.exp(scores - highest[..., None])
    raised_own = jnp.exp(own_score - highest)
    normalizer = jnp.sum(raised, axis=-1) + raised_own
    attn_prob = (raised / normalizer[..., None]).astype(jnp.bfloat16)
    prob_own = (raised_own / normalizer).astype(jnp.bfloat16)
    attended = jnp.einsum(
        "rgql,rlgd->rgqd", attn_prob, resident_values, preferred_element_type=jnp.float32
    )
    attended = (
        attended
        + prob_own.astype(jnp.float32)[..., None]
        * new_token_value.astype(jnp.float32)[:, :, None, :]
    )
    return attended.reshape(count_of_rows, QUERY_HEADS * HEAD_SIZE)


def expert_gate(every_row, router_weight, choices, overflow, my_expert):
    logits = jnp.dot(every_row, router_weight, preferred_element_type=jnp.float32)
    labels = jnp.arange(router_weight.shape[1])
    first_pick = (choices[:, 0:1] == labels[None, :]).astype(jnp.float32)
    second = (choices[:, 1:2] == labels[None, :]).astype(jnp.float32)
    first_logit = jnp.sum(logits * first_pick, axis=-1)
    second_logit = jnp.sum(logits * second, axis=-1)
    first_prob = 1.0 / (1.0 + jnp.exp(second_logit - first_logit))
    kept_share = first_prob * (1.0 - overflow.astype(jnp.float32))
    own_mask = (labels == my_expert).astype(jnp.float32)[None, :]
    return kept_share * jnp.sum(first_pick * own_mask, axis=-1) + (1.0 - kept_share) * jnp.sum(
        second * own_mask, axis=-1
    )


def shards(
    resid,
    query,
    cache,
    new_key_value,
    lengths,
    norm_gain,
    router_weight,
    choices,
    overflow,
    up_weight,
    down_weight,
):
    attended = attend(query, cache, new_key_value, lengths)
    stream = (resid.astype(jnp.float32) + attended).astype(jnp.bfloat16)
    levels = stream.astype(jnp.float32)
    normed = (
        levels * lax.rsqrt(jnp.mean(levels * levels, axis=-1, keepdims=True) + 1e-05) * norm_gain
    ).astype(jnp.bfloat16)
    every_row = lax.all_gather(normed, ("fsdp", "expert", "tensor"), axis=0, tiled=True)
    my_expert = lax.axis_index("expert")
    gate_mine = expert_gate(every_row, router_weight, choices, overflow, my_expert)
    features = up_weight.shape[2]
    my_features = lax.dynamic_slice_in_dim(
        every_row, lax.axis_index("fsdp") * features, features, axis=1
    )
    partial_active = lax.dot_general(
        my_features, up_weight[0], (((1,), (1,)), ((), ())), preferred_element_type=jnp.float32
    )
    pre_active = lax.psum_scatter(partial_active, "fsdp", scatter_dimension=1, tiled=True)
    active = jax.nn.silu(pre_active).astype(jnp.bfloat16)
    partial_value = jnp.dot(
        lax.all_gather(active, "fsdp", axis=1, tiled=True),
        down_weight[0],
        preferred_element_type=jnp.float32,
    )
    weighted = gate_mine[:, None] * partial_value
    combined = lax.psum_scatter(weighted, ("expert", "tensor"), scatter_dimension=0, tiled=True)
    return (stream, combined.astype(jnp.bfloat16))


MESH = pl.DeviceIdType.MESH
GROUPS, FSDP, EXPERTS, CORES = 2, 2, 4, 2
PLANE = FSDP * EXPERTS
BLOCKS = GROUPS * CORES
ROWS = BLOCKS * PLANE
UP_CHUNKS = 4
OUT_CHUNKS = 3


def place_of(slot):
    block, inner = divmod(slot, PLANE)
    group, core = divmod(block, CORES)
    row = inner * CORES + core
    expert_to, rest = divmod(row, 4)
    core_to, pair = divmod(rest, 2)
    return group * 16 + core_to * 8 + expert_to * 2 + pair


def layer_kernel(
    lengths_at,
    choices_at,
    overflow_at,
    resid_at,
    query_at,
    new_kv_at,
    gain_at,
    cache,
    router,
    up,
    down,
    stream_out,
    moe_out,
    lengths,
    choices,
    overflow,
    resid,
    query,
    new_kv,
    gain,
    kv,
    rt,
    upw,
    downw,
    qbd,
    r48,
    payload,
    rows_in,
    rows_all,
    xs,
    x,
    meta,
    logit_mine,
    logit_in,
    pre_mine,
    pre_send,
    pre_in,
    act,
    acc,
    own_out,
    a_send,
    a_in,
    z_send,
    z_in,
    local_sem,
    up_sem,
    down_sem,
    row_send_sem,
    row_recv_sem,
    block_send_sem,
    block_recv_sem,
    pair_send_sem,
    pair_recv_sem,
    pre_send_sem,
    pre_recv_sem,
    a_send_sem,
    a_recv_sem,
    z_send_sem,
    z_recv_sem,
):
    g = lax.axis_index("groups")
    f = lax.axis_index("fsdp")
    e = lax.axis_index("expert")
    t = lax.axis_index("tensor")
    here = f * EXPERTS + e
    block = g * CORES + t
    features = x.shape[1]
    pieces = features // HEAD_SIZE
    heads = 2 * pieces
    group_heads = heads // KEY_VALUE_HEADS
    hidden = upw.shape[1]
    width = moe_out.shape[1] // OUT_CHUNKS
    half = width // 2

    def remote(src, dst, send, recv, device):
        return pltpu.make_async_remote_copy(
            src_ref=src,
            dst_ref=dst,
            send_sem=send,
            recv_sem=recv,
            device_id=device,
            device_id_type=MESH,
        )

    def plane_peer(k):
        other = lax.rem(here + k, PLANE)
        return other // EXPERTS, lax.rem(other, EXPERTS)

    def block_peer(k):
        other = lax.rem(block + k, BLOCKS)
        return other, other // CORES, lax.rem(other, CORES)

    wanted = (
        (query_at, query),
        (cache.at[0, 0], kv.at[0]),
        (lengths_at, lengths),
        (new_kv_at, new_kv),
        (cache.at[1, 0], kv.at[1]),
        (resid_at, resid),
        (gain_at, gain),
        (choices_at, choices),
        (overflow_at, overflow),
        (router.at[:, pl.ds(pl.multiple_of(f * features, features), features)], rt),
    )
    small_copies = [
        pltpu.make_async_copy(src, dst, local_sem.at[i]) for i, (src, dst) in enumerate(wanted)
    ]
    for copy in small_copies:
        copy.start()
    (
        query_copy,
        key_copy,
        lengths_copy,
        new_copy,
        value_copy,
        resid_copy,
        gain_copy,
        choices_copy,
        overflow_copy,
        router_copy,
    ) = small_copies

    barrier = pltpu.get_barrier_semaphore()
    for k in range(1, PLANE):
        f2, e2 = plane_peer(k)
        pl.semaphore_signal(barrier, inc=1, device_id=(g, f2, e2, t), device_id_type=MESH)
    for k in range(1, BLOCKS):
        _, g2, t2 = block_peer(k)
        pl.semaphore_signal(barrier, inc=1, device_id=(g2, f, e, t2), device_id_type=MESH)

    def up_copy(c):
        start = pl.multiple_of(g * (UP_CHUNKS * hidden) + c * hidden, hidden)
        return pltpu.make_async_copy(up.at[0, pl.ds(start, hidden), :], upw.at[c], up_sem.at[c])

    def down_copy(c):
        start = pl.multiple_of(g * (UP_CHUNKS * hidden) + c * hidden, hidden)
        return pltpu.make_async_copy(
            down.at[0, pl.ds(start, hidden), :],
            downw.at[pl.ds(c * hidden, hidden), :],
            down_sem.at[c],
        )

    for c in range(UP_CHUNKS):
        up_copy(c).start()
    for c in range(UP_CHUNKS):
        down_copy(c).start()

    qbd[...] = jnp.zeros_like(qbd)
    query_copy.wait()
    resid_copy.wait()
    query_row = query[...].astype(jnp.float32)
    resid_row = resid[...].astype(jnp.float32)
    for h in range(heads):
        kv_at = h // group_heads * HEAD_SIZE
        qbd[h : h + 1, kv_at : kv_at + HEAD_SIZE] = query_row[:, h * HEAD_SIZE : (h + 1) * HEAD_SIZE]
        r48[h : h + 1, :] = resid_row[:, h * HEAD_SIZE : (h + 1) * HEAD_SIZE]
    inv_root = 1.0 / math.sqrt(HEAD_SIZE)
    new_copy.wait()
    new_rows = new_kv[...].astype(jnp.float32)
    new_key, new_value = new_rows[0:1], new_rows[1:2]
    spread = qbd[...]
    own_score = jnp.sum(spread * new_key, axis=-1, keepdims=True) * inv_root
    spread = spread.astype(jnp.bfloat16)
    key_copy.wait()
    lengths_copy.wait()
    scores = (
        lax.dot_general(
            spread, kv[0], (((1,), (1,)), ((), ())), preferred_element_type=jnp.float32
        )
        * inv_root
    )
    position = lax.broadcasted_iota(jnp.int32, scores.shape, 1)
    scores = jnp.where(position < lengths[0], scores, -1e30)
    highest = jnp.maximum(jnp.max(scores, axis=-1, keepdims=True), own_score)
    raised = jnp.exp(scores - highest)
    raised_own = jnp.exp(own_score - highest)
    normalizer = jnp.sum(raised, axis=-1, keepdims=True) + raised_own
    attn_prob = (raised / normalizer).astype(jnp.bfloat16)
    prob_own = (raised_own / normalizer).astype(jnp.bfloat16).astype(jnp.float32)
    value_copy.wait()
    mixed = jnp.dot(attn_prob, kv[1], preferred_element_type=jnp.float32) + prob_own * new_value
    head_at = lax.broadcasted_iota(jnp.int32, (heads, HEAD_SIZE), 0)
    attended = mixed[:, :HEAD_SIZE]
    for group in range(1, KEY_VALUE_HEADS):
        attended = jnp.where(
            head_at >= group * group_heads,
            mixed[:, group * HEAD_SIZE : (group + 1) * HEAD_SIZE],
            attended,
        )
    levels = (r48[...] + attended).astype(jnp.bfloat16).astype(jnp.float32)
    gain_copy.wait()
    total = jnp.sum(jnp.sum(levels * levels, axis=1, keepdims=True), axis=0, keepdims=True)
    normed = levels * lax.rsqrt(total / (heads * HEAD_SIZE) + 1e-05) * gain[...]
    filler = jnp.zeros((payload.shape[1] - pieces, HEAD_SIZE), jnp.float32)
    for part in range(FSDP):
        payload[part] = jnp.concatenate(
            [normed[part * pieces : (part + 1) * pieces], filler], axis=0
        ).astype(jnp.bfloat16)

    pl.semaphore_wait(barrier, PLANE - 1 + BLOCKS - 1)

    row_copies = []
    for k in range(1, PLANE):
        f2, e2 = plane_peer(k)
        row_copies.append(
            remote(
                payload.at[f2],
                rows_in.at[here],
                row_send_sem.at[k - 1],
                row_recv_sem.at[k - 1],
                (g, f2, e2, t),
            )
        )
        row_copies[-1].start()
    rows_in[here] = payload[f]

    for h in range(heads):
        stream_out[:, h * HEAD_SIZE : (h + 1) * HEAD_SIZE] = levels[h : h + 1].astype(jnp.bfloat16)

    choices_copy.wait()
    overflow_copy.wait()
    at = lax.broadcasted_iota(jnp.int32, (16, HEAD_SIZE), 0)
    lane = lax.broadcasted_iota(jnp.int32, (16, HEAD_SIZE), 1)
    facts = jnp.zeros((16, HEAD_SIZE), jnp.float32)
    for row in range(16):
        place = row % 4 // 2 * 8 + row // 4 * 2 + row % 2
        for col, value in enumerate((choices[0, row], choices[1, row], overflow[row])):
            facts = jnp.where((at == place) & (lane == col), value.astype(jnp.float32), facts)
    meta[g] = facts
    meta_copy = remote(
        meta.at[g], meta.at[g], pair_send_sem.at[0], pair_recv_sem.at[0], (1 - g, f, e, t)
    )
    meta_copy.start()

    for copy in row_copies:
        copy.wait_recv()
    mine = rows_in[...].astype(jnp.float32)[:, :pieces]
    rows_all[block] = mine.reshape(PLANE * pieces, HEAD_SIZE).astype(jnp.bfloat16)
    block_copies = []
    for k in range(1, BLOCKS):
        _, g2, t2 = block_peer(k)
        block_copies.append(
            remote(
                rows_all.at[block],
                rows_all.at[block],
                block_send_sem.at[k - 1],
                block_recv_sem.at[k - 1],
                (g2, f, e, t2),
            )
        )
        block_copies[-1].start()
    for copy in block_copies:
        copy.wait_recv()

    for b in range(BLOCKS):
        taken = rows_all[b].astype(jnp.float32)
        for i in range(PLANE):
            to = place_of(b * PLANE + i) * pieces
            xs[to : to + pieces, :] = taken[i * pieces : (i + 1) * pieces]
    for j in range(pieces):
        x[:, j * HEAD_SIZE : (j + 1) * HEAD_SIZE] = xs[pl.ds(j, ROWS, stride=pieces), :].astype(
            jnp.bfloat16
        )

    across = (g, 1 - f, e, t)
    router_copy.wait()
    labels = rt.shape[0]
    logit_mine[...] = jnp.zeros_like(logit_mine)
    logit_mine[:, :labels] = lax.dot_general(
        x[...], rt[...], (((1,), (1,)), ((), ())), preferred_element_type=jnp.float32
    )
    logit_copy = remote(logit_mine, logit_in, pair_send_sem.at[1], pair_recv_sem.at[1], across)
    logit_copy.start()

    def pre_copy(c):
        return remote(
            pre_send.at[c], pre_in.at[c], pre_send_sem.at[c], pre_recv_sem.at[c], across
        )

    def up_step(c, carry):
        up_copy(c).wait()
        partial = lax.dot_general(
            x[...], upw[c], (((1,), (1,)), ((), ())), preferred_element_type=jnp.float32
        )
        pre_mine[c] = partial
        pre_send[c] = partial.astype(jnp.bfloat16)
        pre_copy(c).start()
        return carry

    lax.fori_loop(0, UP_CHUNKS, up_step, 0)

    meta_copy.wait_recv()
    logit_copy.wait_recv()
    logits = logit_mine[...] + logit_in[...]
    named = jnp.concatenate([meta[0], meta[1]], axis=0)
    label = lax.broadcasted_iota(jnp.int32, logits.shape, 1).astype(jnp.float32)
    first, second, full = named[:, 0:1], named[:, 1:2], named[:, 2:3]
    first_logit = jnp.sum(jnp.where(label == first, logits, 0.0), axis=1, keepdims=True)
    second_logit = jnp.sum(jnp.where(label == second, logits, 0.0), axis=1, keepdims=True)
    first_prob = 1.0 / (1.0 + jnp.exp(second_logit - first_logit))
    kept = first_prob * (1.0 - full)
    my_label = e.astype(jnp.float32)
    gate = jnp.where(first == my_label, kept, 0.0) + jnp.where(second == my_label, 1.0 - kept, 0.0)

    for c in range(UP_CHUNKS):
        down_copy(c).wait()

    def activate(c):
        pre_copy(c).wait_recv()
        value = pre_mine[c] + pre_in[c].astype(jnp.float32)
        act[:, c * hidden : (c + 1) * hidden] = (value / (1.0 + jnp.exp(-value))).astype(
            jnp.bfloat16
        )

    split = UP_CHUNKS // 2 * hidden
    for c in range(UP_CHUNKS // 2):
        activate(c)
    for n in range(OUT_CHUNKS):
        cols = slice(n * width, (n + 1) * width)
        acc[:, cols] = jnp.dot(
            act[:, :split], downw[:split, cols], preferred_element_type=jnp.float32
        )
    for c in range(UP_CHUNKS // 2, UP_CHUNKS):
        activate(c)

    a_copies = [[] for _ in range(OUT_CHUNKS)]
    z_copies = [[] for _ in range(OUT_CHUNKS)]

    def multiply(n):
        cols = slice(n * width, (n + 1) * width)
        value = gate * (
            acc[:, cols]
            + jnp.dot(act[:, split:], downw[split:, cols], preferred_element_type=jnp.float32)
        )
        for b in range(BLOCKS):
            rows = value[b * PLANE : (b + 1) * PLANE]
            folded = jnp.concatenate([rows[:, :half], rows[:, half:]], axis=0)
            own_out[b] = folded
            a_send[n, b] = folded.astype(jnp.bfloat16)
        acc[0:16, n * width : n * width + half] = own_out[block]
        for k in range(1, BLOCKS):
            b2, g2, t2 = block_peer(k)
            at_sem = n * (BLOCKS - 1) + k - 1
            a_copies[n].append(
                remote(
                    a_send.at[n, b2],
                    a_in.at[n, k - 1],
                    a_send_sem.at[at_sem],
                    a_recv_sem.at[at_sem],
                    (g2, f, e, t2),
                )
            )
            a_copies[n][-1].start()

    def add_blocks(n):
        value = acc[0:16, n * width : n * width + half]
        for k in range(1, BLOCKS):
            a_copies[n][k - 1].wait_recv()
            value = value + a_in[n, k - 1].astype(jnp.float32)
        for to in range(EXPERTS):
            z_send[n, to, :, :half] = value[2 * to : 2 * to + 2]
            z_send[n, to, :, half:] = value[PLANE + 2 * to : PLANE + 2 * to + 2]
        for k in range(1, EXPERTS):
            e2 = lax.rem(e + k, EXPERTS)
            at_sem = n * (EXPERTS - 1) + k - 1
            z_copies[n].append(
                remote(
                    z_send.at[n, e2],
                    z_in.at[n, k - 1],
                    z_send_sem.at[at_sem],
                    z_recv_sem.at[at_sem],
                    (g, f, e2, t),
                )
            )
            z_copies[n][-1].start()

    for n in range(OUT_CHUNKS):
        multiply(n)
        if n > 0:
            add_blocks(n - 1)
    add_blocks(OUT_CHUNKS - 1)
    for n in range(OUT_CHUNKS):
        value = z_send[n, e]
        for k in range(1, EXPERTS):
            z_copies[n][k - 1].wait_recv()
            value = value + z_in[n, k - 1]
        moe_out[:, n * width : (n + 1) * width] = value.astype(jnp.bfloat16)

    for copy in row_copies + block_copies + [meta_copy, logit_copy]:
        copy.wait_send()
    for c in range(UP_CHUNKS):
        pre_copy(c).wait_send()
    for n in range(OUT_CHUNKS):
        for copy in a_copies[n] + z_copies[n]:
            copy.wait_send()


def kernel_shards(
    resid,
    query,
    cache,
    new_key_value,
    lengths,
    norm_gain,
    router_weight,
    choices,
    overflow,
    up_weight,
    down_weight,
):
    _, hidden_all, features = up_weight.shape
    hidden = hidden_all // GROUPS
    chunk = hidden // UP_CHUNKS
    width = features // OUT_CHUNKS
    pieces = features // HEAD_SIZE
    padded = -(-pieces // 16) * 16
    heads = FSDP * pieces
    kv_features = cache.shape[3]
    f32, bf16 = jnp.float32, jnp.bfloat16
    vmem = pl.BlockSpec(memory_space=pltpu.VMEM)
    hbm = pl.BlockSpec(memory_space=pltpu.HBM)
    dma = pltpu.SemaphoreType.DMA
    return pl.pallas_call(
        layer_kernel,
        out_shape=(
            jax.ShapeDtypeStruct(resid.shape, bf16),
            jax.ShapeDtypeStruct((ROWS // (BLOCKS * EXPERTS), features), bf16),
        ),
        in_specs=[hbm] * 11,
        out_specs=(vmem, vmem),
        scratch_shapes=[
            pltpu.SMEM(lengths.shape, jnp.int32),
            pltpu.SMEM(choices.shape[::-1], jnp.int32),
            pltpu.SMEM(overflow.shape, jnp.int32),
            pltpu.VMEM(resid.shape, bf16),
            pltpu.VMEM(query.shape, bf16),
            pltpu.VMEM((2, kv_features), bf16),
            pltpu.VMEM((heads, HEAD_SIZE), f32),
            pltpu.VMEM((2, CACHE_POSITIONS, kv_features), bf16),
            pltpu.VMEM((router_weight.shape[1], features), bf16),
            pltpu.VMEM((UP_CHUNKS, chunk, features), bf16),
            pltpu.VMEM((hidden, features), bf16),
            pltpu.VMEM((heads, kv_features), f32),
            pltpu.VMEM((heads, HEAD_SIZE), f32),
            pltpu.VMEM((FSDP, padded, HEAD_SIZE), bf16),
            pltpu.VMEM((PLANE, padded, HEAD_SIZE), bf16),
            pltpu.VMEM((BLOCKS, PLANE * pieces, HEAD_SIZE), bf16),
            pltpu.VMEM((ROWS * pieces, HEAD_SIZE), f32),
            pltpu.VMEM((ROWS, features), bf16),
            pltpu.VMEM((GROUPS, 16, HEAD_SIZE), f32),
            pltpu.VMEM((ROWS, HEAD_SIZE), f32),
            pltpu.VMEM((ROWS, HEAD_SIZE), f32),
            pltpu.VMEM((UP_CHUNKS, ROWS, chunk), f32),
            pltpu.VMEM((UP_CHUNKS, ROWS, chunk), bf16),
            pltpu.VMEM((UP_CHUNKS, ROWS, chunk), bf16),
            pltpu.VMEM((ROWS, hidden), bf16),
            pltpu.VMEM((ROWS, features), f32),
            pltpu.VMEM((BLOCKS, 16, width // 2), f32),
            pltpu.VMEM((OUT_CHUNKS, BLOCKS, 16, width // 2), bf16),
            pltpu.VMEM((OUT_CHUNKS, BLOCKS - 1, 16, width // 2), bf16),
            pltpu.VMEM((OUT_CHUNKS, EXPERTS, 2, width), f32),
            pltpu.VMEM((OUT_CHUNKS, EXPERTS - 1, 2, width), f32),
            dma((10,)),
            dma((UP_CHUNKS,)),
            dma((UP_CHUNKS,)),
            dma((PLANE - 1,)),
            dma((PLANE - 1,)),
            dma((BLOCKS - 1,)),
            dma((BLOCKS - 1,)),
            dma((2,)),
            dma((2,)),
            dma((UP_CHUNKS,)),
            dma((UP_CHUNKS,)),
            dma((OUT_CHUNKS * (BLOCKS - 1),)),
            dma((OUT_CHUNKS * (BLOCKS - 1),)),
            dma((OUT_CHUNKS * (EXPERTS - 1),)),
            dma((OUT_CHUNKS * (EXPERTS - 1),)),
        ],
        compiler_params=pltpu.CompilerParams(
            collective_id=0, has_side_effects=True, vmem_limit_bytes=62 * 1024 * 1024
        ),
        cost_estimate=pl.CostEstimate(
            flops=4 * ROWS * hidden * features,
            bytes_accessed=4 * hidden * features,
            transcendentals=ROWS * hidden,
        ),
        name="layer",
    )(
        lengths,
        choices.T,
        overflow,
        resid,
        query,
        new_key_value.reshape(2, kv_features),
        norm_gain.reshape(heads, HEAD_SIZE),
        cache,
        router_weight.T,
        up_weight,
        down_weight,
    )


def solution(mesh):
    sizes = tuple(mesh.shape[name] for name in ("groups", "fsdp", "expert", "tensor"))
    in_kernel = sizes == (GROUPS, FSDP, EXPERTS, CORES)
    return jax.shard_map(
        kernel_shards if in_kernel else shards,
        mesh=mesh,
        in_specs=(
            P(("groups", "fsdp", "expert", "tensor"), None),
            P(("groups", "fsdp", "expert", "tensor"), None),
            P(None, ("groups", "fsdp", "expert", "tensor"), None, None),
            P(None, ("groups", "fsdp", "expert", "tensor"), None),
            P(("groups", "fsdp", "expert", "tensor")),
            P(),
            P(),
            P("groups", None),
            P("groups"),
            P("expert", "tensor", "fsdp"),
            P("expert", "tensor", "fsdp"),
        ),
        out_specs=(
            P(("groups", "fsdp", "expert", "tensor"), None),
            P(("groups", "expert", "tensor"), "fsdp"),
        ),
        check_vma=False,
    )
```

```python
import math

import jax
import jax.numpy as jnp
from jax import lax
from jax.experimental import pallas as pl
from jax.experimental.pallas import tpu as pltpu
from jax.sharding import PartitionSpec as P

QUERY_HEADS = 48
KEY_VALUE_HEADS = 8
HEAD_SIZE = 128
CACHE_POSITIONS = 64


def attend(query, cache, new_key_value, lengths):
    count_of_rows = query.shape[0]
    heads_per_group = QUERY_HEADS // KEY_VALUE_HEADS
    inv_root = 1.0 / math.sqrt(HEAD_SIZE)
    query_rows = query.reshape(count_of_rows, KEY_VALUE_HEADS, heads_per_group, HEAD_SIZE)
    resident_keys = cache[0].reshape(count_of_rows, CACHE_POSITIONS, KEY_VALUE_HEADS, HEAD_SIZE)
    resident_values = cache[1].reshape(count_of_rows, CACHE_POSITIONS, KEY_VALUE_HEADS, HEAD_SIZE)
    new_token_key = new_key_value[0].reshape(count_of_rows, KEY_VALUE_HEADS, HEAD_SIZE)
    new_token_value = new_key_value[1].reshape(count_of_rows, KEY_VALUE_HEADS, HEAD_SIZE)
    scores = (
        jnp.einsum("rgqd,rlgd->rgql", query_rows, resident_keys, preferred_element_type=jnp.float32)
        * inv_root
    )
    own_score = (
        jnp.einsum("rgqd,rgd->rgq", query_rows, new_token_key, preferred_element_type=jnp.float32)
        * inv_root
    )
    visible = jnp.arange(CACHE_POSITIONS)[None, :] < lengths[:, None]
    scores = jnp.where(visible[:, None, None, :], scores, -1e30)
    highest = jnp.maximum(jnp.max(scores, axis=-1), own_score)
    raised = jnp.exp(scores - highest[..., None])
    raised_own = jnp.exp(own_score - highest)
    normalizer = jnp.sum(raised, axis=-1) + raised_own
    attn_prob = (raised / normalizer[..., None]).astype(jnp.bfloat16)
    prob_own = (raised_own / normalizer).astype(jnp.bfloat16)
    attended = jnp.einsum(
        "rgql,rlgd->rgqd", attn_prob, resident_values, preferred_element_type=jnp.float32
    )
    attended = (
        attended
        + prob_own.astype(jnp.float32)[..., None]
        * new_token_value.astype(jnp.float32)[:, :, None, :]
    )
    return attended.reshape(count_of_rows, QUERY_HEADS * HEAD_SIZE)


def expert_gate(every_row, router_weight, choices, overflow, my_expert):
    logits = jnp.dot(every_row, router_weight, preferred_element_type=jnp.float32)
    labels = jnp.arange(router_weight.shape[1])
    first_pick = (choices[:, 0:1] == labels[None, :]).astype(jnp.float32)
    second = (choices[:, 1:2] == labels[None, :]).astype(jnp.float32)
    first_logit = jnp.sum(logits * first_pick, axis=-1)
    second_logit = jnp.sum(logits * second, axis=-1)
    first_prob = 1.0 / (1.0 + jnp.exp(second_logit - first_logit))
    kept_share = first_prob * (1.0 - overflow.astype(jnp.float32))
    own_mask = (labels == my_expert).astype(jnp.float32)[None, :]
    return kept_share * jnp.sum(first_pick * own_mask, axis=-1) + (1.0 - kept_share) * jnp.sum(
        second * own_mask, axis=-1
    )


def shards(
    resid,
    query,
    cache,
    new_key_value,
    lengths,
    norm_gain,
    router_weight,
    choices,
    overflow,
    up_weight,
    down_weight,
):
    attended = attend(query, cache, new_key_value, lengths)
    stream = (resid.astype(jnp.float32) + attended).astype(jnp.bfloat16)
    levels = stream.astype(jnp.float32)
    normed = (
        levels * lax.rsqrt(jnp.mean(levels * levels, axis=-1, keepdims=True) + 1e-05) * norm_gain
    ).astype(jnp.bfloat16)
    every_row = lax.all_gather(normed, ("fsdp", "expert", "tensor"), axis=0, tiled=True)
    my_expert = lax.axis_index("expert")
    gate_mine = expert_gate(every_row, router_weight, choices, overflow, my_expert)
    features = up_weight.shape[2]
    my_features = lax.dynamic_slice_in_dim(
        every_row, lax.axis_index("fsdp") * features, features, axis=1
    )
    partial_active = lax.dot_general(
        my_features, up_weight[0], (((1,), (1,)), ((), ())), preferred_element_type=jnp.float32
    )
    pre_active = lax.psum_scatter(partial_active, "fsdp", scatter_dimension=1, tiled=True)
    active = jax.nn.silu(pre_active).astype(jnp.bfloat16)
    partial_value = jnp.dot(
        lax.all_gather(active, "fsdp", axis=1, tiled=True),
        down_weight[0],
        preferred_element_type=jnp.float32,
    )
    weighted = gate_mine[:, None] * partial_value
    combined = lax.psum_scatter(weighted, ("expert", "tensor"), scatter_dimension=0, tiled=True)
    return (stream, combined.astype(jnp.bfloat16))


MESH = pl.DeviceIdType.MESH
GROUPS, FSDP, EXPERTS, CORES = 2, 2, 4, 2
PLANE = FSDP * EXPERTS
BLOCKS = GROUPS * CORES
ROWS = BLOCKS * PLANE
UP_CHUNKS = 4
OUT_CHUNKS = 3


def place_of(slot):
    block, inner = divmod(slot, PLANE)
    group, core = divmod(block, CORES)
    row = inner * CORES + core
    expert_to, rest = divmod(row, 4)
    core_to, pair = divmod(rest, 2)
    return group * 16 + core_to * 8 + expert_to * 2 + pair


def layer_kernel(
    lengths_at,
    choices_at,
    overflow_at,
    resid_at,
    query_at,
    new_kv_at,
    gain_at,
    cache,
    router,
    up,
    down,
    stream_out,
    moe_out,
    lengths,
    choices,
    overflow,
    resid,
    query,
    new_kv,
    gain,
    kv,
    rt,
    upw,
    downw,
    qbd,
    r48,
    payload,
    rows_in,
    rows_all,
    xs,
    x,
    meta,
    logit_mine,
    logit_in,
    pre_mine,
    pre_send,
    pre_in,
    act,
    acc,
    own_out,
    a_send,
    a_in,
    z_mine,
    z_send,
    z_in,
    local_sem,
    up_sem,
    down_sem,
    row_send_sem,
    row_recv_sem,
    block_send_sem,
    block_recv_sem,
    pair_send_sem,
    pair_recv_sem,
    pre_send_sem,
    pre_recv_sem,
    a_send_sem,
    a_recv_sem,
    z_send_sem,
    z_recv_sem,
):
    g = lax.axis_index("groups")
    f = lax.axis_index("fsdp")
    e = lax.axis_index("expert")
    t = lax.axis_index("tensor")
    here = f * EXPERTS + e
    block = g * CORES + t
    features = x.shape[1]
    pieces = features // HEAD_SIZE
    heads = 2 * pieces
    group_heads = heads // KEY_VALUE_HEADS
    hidden = upw.shape[1]
    width = moe_out.shape[1] // OUT_CHUNKS
    half = width // 2

    def remote(src, dst, send, recv, device):
        return pltpu.make_async_remote_copy(
            src_ref=src,
            dst_ref=dst,
            send_sem=send,
            recv_sem=recv,
            device_id=device,
            device_id_type=MESH,
        )

    def plane_peer(k):
        other = lax.rem(here + k, PLANE)
        return other // EXPERTS, lax.rem(other, EXPERTS)

    def block_peer(k):
        other = lax.rem(block + k, BLOCKS)
        return other, other // CORES, lax.rem(other, CORES)

    wanted = (
        (query_at, query),
        (cache.at[0, 0], kv.at[0]),
        (lengths_at, lengths),
        (new_kv_at, new_kv),
        (cache.at[1, 0], kv.at[1]),
        (resid_at, resid),
        (gain_at, gain),
        (choices_at, choices),
        (overflow_at, overflow),
        (router.at[:, pl.ds(pl.multiple_of(f * features, features), features)], rt),
    )
    small_copies = [
        pltpu.make_async_copy(src, dst, local_sem.at[i]) for i, (src, dst) in enumerate(wanted)
    ]
    for copy in small_copies:
        copy.start()
    (
        query_copy,
        key_copy,
        lengths_copy,
        new_copy,
        value_copy,
        resid_copy,
        gain_copy,
        choices_copy,
        overflow_copy,
        router_copy,
    ) = small_copies

    barrier = pltpu.get_barrier_semaphore()
    for k in range(1, PLANE):
        f2, e2 = plane_peer(k)
        pl.semaphore_signal(barrier, inc=1, device_id=(g, f2, e2, t), device_id_type=MESH)
    for k in range(1, BLOCKS):
        _, g2, t2 = block_peer(k)
        pl.semaphore_signal(barrier, inc=1, device_id=(g2, f, e, t2), device_id_type=MESH)

    def up_copy(c):
        start = pl.multiple_of(g * (UP_CHUNKS * hidden) + c * hidden, hidden)
        return pltpu.make_async_copy(up.at[0, pl.ds(start, hidden), :], upw.at[c], up_sem.at[c])

    def down_copy(c):
        start = pl.multiple_of(g * (UP_CHUNKS * hidden) + c * hidden, hidden)
        return pltpu.make_async_copy(
            down.at[0, pl.ds(start, hidden), :],
            downw.at[pl.ds(c * hidden, hidden), :],
            down_sem.at[c],
        )

    for c in range(UP_CHUNKS):
        up_copy(c).start()
    for c in range(UP_CHUNKS):
        down_copy(c).start()

    qbd[...] = jnp.zeros_like(qbd)
    query_copy.wait()
    resid_copy.wait()
    query_row = query[...].astype(jnp.float32)
    resid_row = resid[...].astype(jnp.float32)
    for h in range(heads):
        kv_at = h // group_heads * HEAD_SIZE
        qbd[h : h + 1, kv_at : kv_at + HEAD_SIZE] = query_row[:, h * HEAD_SIZE : (h + 1) * HEAD_SIZE]
        r48[h : h + 1, :] = resid_row[:, h * HEAD_SIZE : (h + 1) * HEAD_SIZE]
    inv_root = 1.0 / math.sqrt(HEAD_SIZE)
    new_copy.wait()
    new_rows = new_kv[...].astype(jnp.float32)
    new_key, new_value = new_rows[0:1], new_rows[1:2]
    spread = qbd[...]
    own_score = jnp.sum(spread * new_key, axis=-1, keepdims=True) * inv_root
    spread = spread.astype(jnp.bfloat16)
    key_copy.wait()
    lengths_copy.wait()
    scores = (
        lax.dot_general(
            spread, kv[0], (((1,), (1,)), ((), ())), preferred_element_type=jnp.float32
        )
        * inv_root
    )
    position = lax.broadcasted_iota(jnp.int32, scores.shape, 1)
    scores = jnp.where(position < lengths[0], scores, -1e30)
    highest = jnp.maximum(jnp.max(scores, axis=-1, keepdims=True), own_score)
    raised = jnp.exp(scores - highest)
    raised_own = jnp.exp(own_score - highest)
    normalizer = jnp.sum(raised, axis=-1, keepdims=True) + raised_own
    attn_prob = (raised / normalizer).astype(jnp.bfloat16)
    prob_own = (raised_own / normalizer).astype(jnp.bfloat16).astype(jnp.float32)
    value_copy.wait()
    mixed = jnp.dot(attn_prob, kv[1], preferred_element_type=jnp.float32) + prob_own * new_value
    head_at = lax.broadcasted_iota(jnp.int32, (heads, HEAD_SIZE), 0)
    attended = mixed[:, :HEAD_SIZE]
    for group in range(1, KEY_VALUE_HEADS):
        attended = jnp.where(
            head_at >= group * group_heads,
            mixed[:, group * HEAD_SIZE : (group + 1) * HEAD_SIZE],
            attended,
        )
    levels = (r48[...] + attended).astype(jnp.bfloat16).astype(jnp.float32)
    gain_copy.wait()
    total = jnp.sum(jnp.sum(levels * levels, axis=1, keepdims=True), axis=0, keepdims=True)
    normed = levels * lax.rsqrt(total / (heads * HEAD_SIZE) + 1e-05) * gain[...]
    filler = jnp.zeros((payload.shape[1] - pieces, HEAD_SIZE), jnp.float32)
    for part in range(FSDP):
        payload[part] = jnp.concatenate(
            [normed[part * pieces : (part + 1) * pieces], filler], axis=0
        ).astype(jnp.bfloat16)

    pl.semaphore_wait(barrier, PLANE - 1 + BLOCKS - 1)

    row_copies = []
    for k in range(1, PLANE):
        f2, e2 = plane_peer(k)
        row_copies.append(
            remote(
                payload.at[f2],
                rows_in.at[here],
                row_send_sem.at[k - 1],
                row_recv_sem.at[k - 1],
                (g, f2, e2, t),
            )
        )
        row_copies[-1].start()
    rows_in[here] = payload[f]

    for h in range(heads):
        stream_out[:, h * HEAD_SIZE : (h + 1) * HEAD_SIZE] = levels[h : h + 1].astype(jnp.bfloat16)

    choices_copy.wait()
    overflow_copy.wait()
    at = lax.broadcasted_iota(jnp.int32, (16, HEAD_SIZE), 0)
    lane = lax.broadcasted_iota(jnp.int32, (16, HEAD_SIZE), 1)
    facts = jnp.zeros((16, HEAD_SIZE), jnp.float32)
    for row in range(16):
        place = row % 4 // 2 * 8 + row // 4 * 2 + row % 2
        for col, value in enumerate((choices[0, row], choices[1, row], overflow[row])):
            facts = jnp.where((at == place) & (lane == col), value.astype(jnp.float32), facts)
    meta[g] = facts
    meta_copy = remote(
        meta.at[g], meta.at[g], pair_send_sem.at[0], pair_recv_sem.at[0], (1 - g, f, e, t)
    )
    meta_copy.start()

    for copy in row_copies:
        copy.wait_recv()
    mine = rows_in[...].astype(jnp.float32)[:, :pieces]
    rows_all[block] = mine.reshape(PLANE * pieces, HEAD_SIZE).astype(jnp.bfloat16)
    block_copies = []
    for k in range(1, BLOCKS):
        _, g2, t2 = block_peer(k)
        block_copies.append(
            remote(
                rows_all.at[block],
                rows_all.at[block],
                block_send_sem.at[k - 1],
                block_recv_sem.at[k - 1],
                (g2, f, e, t2),
            )
        )
        block_copies[-1].start()
    for copy in block_copies:
        copy.wait_recv()

    for b in range(BLOCKS):
        taken = rows_all[b].astype(jnp.float32)
        for i in range(PLANE):
            to = place_of(b * PLANE + i) * pieces
            xs[to : to + pieces, :] = taken[i * pieces : (i + 1) * pieces]
    for j in range(pieces):
        x[:, j * HEAD_SIZE : (j + 1) * HEAD_SIZE] = xs[pl.ds(j, ROWS, stride=pieces), :].astype(
            jnp.bfloat16
        )

    across = (g, 1 - f, e, t)
    def pre_copy(c):
        return remote(
            pre_send.at[c], pre_in.at[c], pre_send_sem.at[c], pre_recv_sem.at[c], across
        )

    def up_step(c, carry):
        up_copy(c).wait()
        partial = lax.dot_general(
            x[...], upw[c], (((1,), (1,)), ((), ())), preferred_element_type=jnp.float32
        )
        pre_mine[c] = partial
        pre_send[c] = partial.astype(jnp.bfloat16)
        pre_copy(c).start()
        return carry

    up_step(0, 0)
    router_copy.wait()
    labels = rt.shape[0]
    logit_mine[...] = jnp.zeros_like(logit_mine)
    logit_mine[:, :labels] = lax.dot_general(
        x[...], rt[...], (((1,), (1,)), ((), ())), preferred_element_type=jnp.float32
    )
    logit_copy = remote(logit_mine, logit_in, pair_send_sem.at[1], pair_recv_sem.at[1], across)
    logit_copy.start()
    lax.fori_loop(1, UP_CHUNKS, up_step, 0)

    meta_copy.wait_recv()
    logit_copy.wait_recv()
    logits = logit_mine[...] + logit_in[...]
    named = jnp.concatenate([meta[0], meta[1]], axis=0)
    label = lax.broadcasted_iota(jnp.int32, logits.shape, 1).astype(jnp.float32)
    first, second, full = named[:, 0:1], named[:, 1:2], named[:, 2:3]
    first_logit = jnp.sum(jnp.where(label == first, logits, 0.0), axis=1, keepdims=True)
    second_logit = jnp.sum(jnp.where(label == second, logits, 0.0), axis=1, keepdims=True)
    first_prob = 1.0 / (1.0 + jnp.exp(second_logit - first_logit))
    kept = first_prob * (1.0 - full)
    my_label = e.astype(jnp.float32)
    gate = jnp.where(first == my_label, kept, 0.0) + jnp.where(second == my_label, 1.0 - kept, 0.0)

    for c in range(UP_CHUNKS):
        down_copy(c).wait()

    def activate(c):
        pre_copy(c).wait_recv()
        value = pre_mine[c] + pre_in[c].astype(jnp.float32)
        act[:, c * hidden : (c + 1) * hidden] = (value / (1.0 + jnp.exp(-value))).astype(
            jnp.bfloat16
        )

    split = (UP_CHUNKS - 1) * hidden
    for c in range(UP_CHUNKS - 1):
        activate(c)
        rows = slice(c * hidden, (c + 1) * hidden)
        product = jnp.dot(act[:, rows], downw[rows, :], preferred_element_type=jnp.float32)
        acc[...] = product if c == 0 else acc[...] + product
    activate(UP_CHUNKS - 1)

    a_copies = [[] for _ in range(OUT_CHUNKS)]
    z_copies = [[] for _ in range(OUT_CHUNKS)]

    def multiply(n):
        cols = slice(n * width, (n + 1) * width)
        value = gate * (
            acc[:, cols]
            + jnp.dot(act[:, split:], downw[split:, cols], preferred_element_type=jnp.float32)
        )
        for b in range(BLOCKS):
            rows = value[b * PLANE : (b + 1) * PLANE]
            folded = jnp.concatenate([rows[:, :half], rows[:, half:]], axis=0)
            own_out[b] = folded
            a_send[n, b] = folded.astype(jnp.bfloat16)
        acc[0:16, n * width : n * width + half] = own_out[block]
        for k in range(1, BLOCKS):
            b2, g2, t2 = block_peer(k)
            at_sem = n * (BLOCKS - 1) + k - 1
            a_copies[n].append(
                remote(
                    a_send.at[n, b2],
                    a_in.at[n, k - 1],
                    a_send_sem.at[at_sem],
                    a_recv_sem.at[at_sem],
                    (g2, f, e, t2),
                )
            )
            a_copies[n][-1].start()

    def add_blocks(n):
        value = acc[0:16, n * width : n * width + half]
        for k in range(1, BLOCKS):
            a_copies[n][k - 1].wait_recv()
            value = value + a_in[n, k - 1].astype(jnp.float32)
        for to in range(EXPERTS):
            for j in range(width // HEAD_SIZE):
                side, col = divmod(j * HEAD_SIZE, half)
                row = side * PLANE + 2 * to
                z_mine[n, to, 2 * j : 2 * j + 2, :] = value[row : row + 2, col : col + HEAD_SIZE]
            z_send[n, to] = z_mine[n, to].astype(jnp.bfloat16)
        for k in range(1, EXPERTS):
            e2 = lax.rem(e + k, EXPERTS)
            at_sem = n * (EXPERTS - 1) + k - 1
            z_copies[n].append(
                remote(
                    z_send.at[n, e2],
                    z_in.at[n, k - 1],
                    z_send_sem.at[at_sem],
                    z_recv_sem.at[at_sem],
                    (g, f, e2, t),
                )
            )
            z_copies[n][-1].start()

    for n in range(OUT_CHUNKS):
        multiply(n)
    for n in range(OUT_CHUNKS):
        add_blocks(n)
    for n in range(OUT_CHUNKS):
        value = z_mine[n, e]
        for k in range(1, EXPERTS):
            z_copies[n][k - 1].wait_recv()
            value = value + z_in[n, k - 1].astype(jnp.float32)
        for j in range(width // HEAD_SIZE):
            at_col = n * width + j * HEAD_SIZE
            moe_out[:, at_col : at_col + HEAD_SIZE] = value[2 * j : 2 * j + 2].astype(jnp.bfloat16)

    for copy in row_copies + block_copies + [meta_copy, logit_copy]:
        copy.wait_send()
    for c in range(UP_CHUNKS):
        pre_copy(c).wait_send()
    for n in range(OUT_CHUNKS):
        for copy in a_copies[n] + z_copies[n]:
            copy.wait_send()


def kernel_shards(
    resid,
    query,
    cache,
    new_key_value,
    lengths,
    norm_gain,
    router_weight,
    choices,
    overflow,
    up_weight,
    down_weight,
):
    _, hidden_all, features = up_weight.shape
    hidden = hidden_all // GROUPS
    chunk = hidden // UP_CHUNKS
    width = features // OUT_CHUNKS
    fold = 2 * width // HEAD_SIZE
    pieces = features // HEAD_SIZE
    padded = -(-pieces // 16) * 16
    heads = FSDP * pieces
    kv_features = cache.shape[3]
    f32, bf16 = jnp.float32, jnp.bfloat16
    vmem = pl.BlockSpec(memory_space=pltpu.VMEM)
    hbm = pl.BlockSpec(memory_space=pltpu.HBM)
    dma = pltpu.SemaphoreType.DMA
    return pl.pallas_call(
        layer_kernel,
        out_shape=(
            jax.ShapeDtypeStruct(resid.shape, bf16),
            jax.ShapeDtypeStruct((ROWS // (BLOCKS * EXPERTS), features), bf16),
        ),
        in_specs=[hbm] * 11,
        out_specs=(vmem, vmem),
        scratch_shapes=[
            pltpu.SMEM(lengths.shape, jnp.int32),
            pltpu.SMEM(choices.shape[::-1], jnp.int32),
            pltpu.SMEM(overflow.shape, jnp.int32),
            pltpu.VMEM(resid.shape, bf16),
            pltpu.VMEM(query.shape, bf16),
            pltpu.VMEM((2, kv_features), bf16),
            pltpu.VMEM((heads, HEAD_SIZE), f32),
            pltpu.VMEM((2, CACHE_POSITIONS, kv_features), bf16),
            pltpu.VMEM((router_weight.shape[1], features), bf16),
            pltpu.VMEM((UP_CHUNKS, chunk, features), bf16),
            pltpu.VMEM((hidden, features), bf16),
            pltpu.VMEM((heads, kv_features), f32),
            pltpu.VMEM((heads, HEAD_SIZE), f32),
            pltpu.VMEM((FSDP, padded, HEAD_SIZE), bf16),
            pltpu.VMEM((PLANE, padded, HEAD_SIZE), bf16),
            pltpu.VMEM((BLOCKS, PLANE * pieces, HEAD_SIZE), bf16),
            pltpu.VMEM((ROWS * pieces, HEAD_SIZE), f32),
            pltpu.VMEM((ROWS, features), bf16),
            pltpu.VMEM((GROUPS, 16, HEAD_SIZE), f32),
            pltpu.VMEM((ROWS, HEAD_SIZE), f32),
            pltpu.VMEM((ROWS, HEAD_SIZE), f32),
            pltpu.VMEM((UP_CHUNKS, ROWS, chunk), f32),
            pltpu.VMEM((UP_CHUNKS, ROWS, chunk), bf16),
            pltpu.VMEM((UP_CHUNKS, ROWS, chunk), bf16),
            pltpu.VMEM((ROWS, hidden), bf16),
            pltpu.VMEM((ROWS, features), f32),
            pltpu.VMEM((BLOCKS, 16, width // 2), f32),
            pltpu.VMEM((OUT_CHUNKS, BLOCKS, 16, width // 2), bf16),
            pltpu.VMEM((OUT_CHUNKS, BLOCKS - 1, 16, width // 2), bf16),
            pltpu.VMEM((OUT_CHUNKS, EXPERTS, fold, HEAD_SIZE), f32),
            pltpu.VMEM((OUT_CHUNKS, EXPERTS, fold, HEAD_SIZE), bf16),
            pltpu.VMEM((OUT_CHUNKS, EXPERTS - 1, fold, HEAD_SIZE), bf16),
            dma((10,)),
            dma((UP_CHUNKS,)),
            dma((UP_CHUNKS,)),
            dma((PLANE - 1,)),
            dma((PLANE - 1,)),
            dma((BLOCKS - 1,)),
            dma((BLOCKS - 1,)),
            dma((2,)),
            dma((2,)),
            dma((UP_CHUNKS,)),
            dma((UP_CHUNKS,)),
            dma((OUT_CHUNKS * (BLOCKS - 1),)),
            dma((OUT_CHUNKS * (BLOCKS - 1),)),
            dma((OUT_CHUNKS * (EXPERTS - 1),)),
            dma((OUT_CHUNKS * (EXPERTS - 1),)),
        ],
        compiler_params=pltpu.CompilerParams(
            collective_id=0, has_side_effects=True, vmem_limit_bytes=62 * 1024 * 1024
        ),
        cost_estimate=pl.CostEstimate(
            flops=4 * ROWS * hidden * features,
            bytes_accessed=4 * hidden * features,
            transcendentals=ROWS * hidden,
        ),
        name="layer",
    )(
        lengths,
        choices.T,
        overflow,
        resid,
        query,
        new_key_value.reshape(2, kv_features),
        norm_gain.reshape(heads, HEAD_SIZE),
        cache,
        router_weight.T,
        up_weight,
        down_weight,
    )


def solution(mesh):
    sizes = tuple(mesh.shape[name] for name in ("groups", "fsdp", "expert", "tensor"))
    in_kernel = sizes == (GROUPS, FSDP, EXPERTS, CORES)
    return jax.shard_map(
        kernel_shards if in_kernel else shards,
        mesh=mesh,
        in_specs=(
            P(("groups", "fsdp", "expert", "tensor"), None),
            P(("groups", "fsdp", "expert", "tensor"), None),
            P(None, ("groups", "fsdp", "expert", "tensor"), None, None),
            P(None, ("groups", "fsdp", "expert", "tensor"), None),
            P(("groups", "fsdp", "expert", "tensor")),
            P(),
            P(),
            P("groups", None),
            P("groups"),
            P("expert", "tensor", "fsdp"),
            P("expert", "tensor", "fsdp"),
        ),
        out_specs=(
            P(("groups", "fsdp", "expert", "tensor"), None),
            P(("groups", "expert", "tensor"), "fsdp"),
        ),
        check_vma=False,
    )
```

```python
import math

import jax
import jax.numpy as jnp
from jax import lax
from jax.experimental import pallas as pl
from jax.experimental.pallas import tpu as pltpu
from jax.sharding import PartitionSpec as P

QUERY_HEADS = 48
KEY_VALUE_HEADS = 8
HEAD_SIZE = 128
CACHE_POSITIONS = 64


def attend(query, cache, new_key_value, lengths):
    count_of_rows = query.shape[0]
    heads_per_group = QUERY_HEADS // KEY_VALUE_HEADS
    inv_root = 1.0 / math.sqrt(HEAD_SIZE)
    query_rows = query.reshape(count_of_rows, KEY_VALUE_HEADS, heads_per_group, HEAD_SIZE)
    resident_keys = cache[0].reshape(count_of_rows, CACHE_POSITIONS, KEY_VALUE_HEADS, HEAD_SIZE)
    resident_values = cache[1].reshape(count_of_rows, CACHE_POSITIONS, KEY_VALUE_HEADS, HEAD_SIZE)
    new_token_key = new_key_value[0].reshape(count_of_rows, KEY_VALUE_HEADS, HEAD_SIZE)
    new_token_value = new_key_value[1].reshape(count_of_rows, KEY_VALUE_HEADS, HEAD_SIZE)
    scores = (
        jnp.einsum("rgqd,rlgd->rgql", query_rows, resident_keys, preferred_element_type=jnp.float32)
        * inv_root
    )
    own_score = (
        jnp.einsum("rgqd,rgd->rgq", query_rows, new_token_key, preferred_element_type=jnp.float32)
        * inv_root
    )
    visible = jnp.arange(CACHE_POSITIONS)[None, :] < lengths[:, None]
    scores = jnp.where(visible[:, None, None, :], scores, -1e30)
    highest = jnp.maximum(jnp.max(scores, axis=-1), own_score)
    raised = jnp.exp(scores - highest[..., None])
    raised_own = jnp.exp(own_score - highest)
    normalizer = jnp.sum(raised, axis=-1) + raised_own
    attn_prob = (raised / normalizer[..., None]).astype(jnp.bfloat16)
    prob_own = (raised_own / normalizer).astype(jnp.bfloat16)
    attended = jnp.einsum(
        "rgql,rlgd->rgqd", attn_prob, resident_values, preferred_element_type=jnp.float32
    )
    attended = (
        attended
        + prob_own.astype(jnp.float32)[..., None]
        * new_token_value.astype(jnp.float32)[:, :, None, :]
    )
    return attended.reshape(count_of_rows, QUERY_HEADS * HEAD_SIZE)


def expert_gate(every_row, router_weight, choices, overflow, my_expert):
    logits = jnp.dot(every_row, router_weight, preferred_element_type=jnp.float32)
    labels = jnp.arange(router_weight.shape[1])
    first_pick = (choices[:, 0:1] == labels[None, :]).astype(jnp.float32)
    second = (choices[:, 1:2] == labels[None, :]).astype(jnp.float32)
    first_logit = jnp.sum(logits * first_pick, axis=-1)
    second_logit = jnp.sum(logits * second, axis=-1)
    first_prob = 1.0 / (1.0 + jnp.exp(second_logit - first_logit))
    kept_share = first_prob * (1.0 - overflow.astype(jnp.float32))
    own_mask = (labels == my_expert).astype(jnp.float32)[None, :]
    return kept_share * jnp.sum(first_pick * own_mask, axis=-1) + (1.0 - kept_share) * jnp.sum(
        second * own_mask, axis=-1
    )


def shards(
    resid,
    query,
    cache,
    new_key_value,
    lengths,
    norm_gain,
    router_weight,
    choices,
    overflow,
    up_weight,
    down_weight,
):
    attended = attend(query, cache, new_key_value, lengths)
    stream = (resid.astype(jnp.float32) + attended).astype(jnp.bfloat16)
    levels = stream.astype(jnp.float32)
    normed = (
        levels * lax.rsqrt(jnp.mean(levels * levels, axis=-1, keepdims=True) + 1e-05) * norm_gain
    ).astype(jnp.bfloat16)
    every_row = lax.all_gather(normed, ("fsdp", "expert", "tensor"), axis=0, tiled=True)
    my_expert = lax.axis_index("expert")
    gate_mine = expert_gate(every_row, router_weight, choices, overflow, my_expert)
    features = up_weight.shape[2]
    my_features = lax.dynamic_slice_in_dim(
        every_row, lax.axis_index("fsdp") * features, features, axis=1
    )
    partial_active = lax.dot_general(
        my_features, up_weight[0], (((1,), (1,)), ((), ())), preferred_element_type=jnp.float32
    )
    pre_active = lax.psum_scatter(partial_active, "fsdp", scatter_dimension=1, tiled=True)
    active = jax.nn.silu(pre_active).astype(jnp.bfloat16)
    partial_value = jnp.dot(
        lax.all_gather(active, "fsdp", axis=1, tiled=True),
        down_weight[0],
        preferred_element_type=jnp.float32,
    )
    weighted = gate_mine[:, None] * partial_value
    combined = lax.psum_scatter(weighted, ("expert", "tensor"), scatter_dimension=0, tiled=True)
    return (stream, combined.astype(jnp.bfloat16))


MESH = pl.DeviceIdType.MESH
GROUPS, FSDP, EXPERTS, CORES = 2, 2, 4, 2
PLANE = FSDP * EXPERTS
BLOCKS = GROUPS * CORES
ROWS = BLOCKS * PLANE
UP_CHUNKS = 4
OUT_CHUNKS = 3


def place_of(slot):
    block, inner = divmod(slot, PLANE)
    group, core = divmod(block, CORES)
    row = inner * CORES + core
    expert_to, rest = divmod(row, 4)
    core_to, pair = divmod(rest, 2)
    return group * 16 + core_to * 8 + expert_to * 2 + pair


def layer_kernel(
    lengths_at,
    choices_at,
    overflow_at,
    resid_at,
    query_at,
    new_kv_at,
    gain_at,
    cache,
    router,
    up,
    down,
    both_out,
    lengths,
    choices,
    overflow,
    resid,
    query,
    new_kv,
    gain,
    kv,
    rt,
    upw,
    downw,
    qbd,
    r48,
    payload,
    rows_in,
    rows_all,
    xs,
    x,
    meta,
    logit_mine,
    logit_in,
    pre_mine,
    pre_send,
    pre_in,
    act,
    acc,
    own_out,
    a_send,
    a_in,
    z_mine,
    z_send,
    z_in,
    local_sem,
    up_sem,
    down_sem,
    row_send_sem,
    row_recv_sem,
    block_send_sem,
    block_recv_sem,
    pair_send_sem,
    pair_recv_sem,
    pre_send_sem,
    pre_recv_sem,
    a_send_sem,
    a_recv_sem,
    z_send_sem,
    z_recv_sem,
):
    g = lax.axis_index("groups")
    f = lax.axis_index("fsdp")
    e = lax.axis_index("expert")
    t = lax.axis_index("tensor")
    here = f * EXPERTS + e
    block = g * CORES + t
    features = x.shape[1]
    pieces = features // HEAD_SIZE
    heads = 2 * pieces
    group_heads = heads // KEY_VALUE_HEADS
    hidden = upw.shape[1]
    width = features // OUT_CHUNKS
    half = width // 2

    def remote(src, dst, send, recv, device):
        return pltpu.make_async_remote_copy(
            src_ref=src,
            dst_ref=dst,
            send_sem=send,
            recv_sem=recv,
            device_id=device,
            device_id_type=MESH,
        )

    def plane_peer(k):
        other = lax.rem(here + k, PLANE)
        return other // EXPERTS, lax.rem(other, EXPERTS)

    def block_peer(k):
        other = lax.rem(block + k, BLOCKS)
        return other, other // CORES, lax.rem(other, CORES)

    wanted = (
        (query_at, query),
        (cache.at[0, 0], kv.at[0]),
        (lengths_at, lengths),
        (new_kv_at, new_kv),
        (cache.at[1, 0], kv.at[1]),
        (resid_at, resid),
        (gain_at, gain),
        (choices_at, choices),
        (overflow_at, overflow),
        (router.at[:, pl.ds(pl.multiple_of(f * features, features), features)], rt),
    )
    small_copies = [
        pltpu.make_async_copy(src, dst, local_sem.at[i]) for i, (src, dst) in enumerate(wanted)
    ]
    for copy in small_copies:
        copy.start()
    (
        query_copy,
        key_copy,
        lengths_copy,
        new_copy,
        value_copy,
        resid_copy,
        gain_copy,
        choices_copy,
        overflow_copy,
        router_copy,
    ) = small_copies

    barrier = pltpu.get_barrier_semaphore()
    for k in range(1, PLANE):
        f2, e2 = plane_peer(k)
        pl.semaphore_signal(barrier, inc=1, device_id=(g, f2, e2, t), device_id_type=MESH)
    for k in range(1, BLOCKS):
        _, g2, t2 = block_peer(k)
        pl.semaphore_signal(barrier, inc=1, device_id=(g2, f, e, t2), device_id_type=MESH)

    def up_copy(c):
        start = pl.multiple_of(g * (UP_CHUNKS * hidden) + c * hidden, hidden)
        return pltpu.make_async_copy(up.at[0, pl.ds(start, hidden), :], upw.at[c], up_sem.at[c])

    def down_copy(c):
        start = pl.multiple_of(g * (UP_CHUNKS * hidden) + c * hidden, hidden)
        return pltpu.make_async_copy(
            down.at[0, pl.ds(start, hidden), :],
            downw.at[pl.ds(c * hidden, hidden), :],
            down_sem.at[c],
        )

    for c in range(UP_CHUNKS):
        up_copy(c).start()
    for c in range(UP_CHUNKS):
        down_copy(c).start()

    qbd[...] = jnp.zeros_like(qbd)
    query_copy.wait()
    resid_copy.wait()
    query_row = query[...].astype(jnp.float32)
    resid_row = resid[...].astype(jnp.float32)
    for h in range(heads):
        kv_at = h // group_heads * HEAD_SIZE
        qbd[h : h + 1, kv_at : kv_at + HEAD_SIZE] = query_row[:, h * HEAD_SIZE : (h + 1) * HEAD_SIZE]
        r48[h : h + 1, :] = resid_row[:, h * HEAD_SIZE : (h + 1) * HEAD_SIZE]
    inv_root = 1.0 / math.sqrt(HEAD_SIZE)
    new_copy.wait()
    new_rows = new_kv[...].astype(jnp.float32)
    new_key, new_value = new_rows[0:1], new_rows[1:2]
    spread = qbd[...]
    own_score = jnp.sum(spread * new_key, axis=-1, keepdims=True) * inv_root
    spread = spread.astype(jnp.bfloat16)
    key_copy.wait()
    lengths_copy.wait()
    scores = (
        lax.dot_general(
            spread, kv[0], (((1,), (1,)), ((), ())), preferred_element_type=jnp.float32
        )
        * inv_root
    )
    position = lax.broadcasted_iota(jnp.int32, scores.shape, 1)
    scores = jnp.where(position < lengths[0], scores, -1e30)
    highest = jnp.maximum(jnp.max(scores, axis=-1, keepdims=True), own_score)
    raised = jnp.exp(scores - highest)
    raised_own = jnp.exp(own_score - highest)
    normalizer = jnp.sum(raised, axis=-1, keepdims=True) + raised_own
    attn_prob = (raised / normalizer).astype(jnp.bfloat16)
    prob_own = (raised_own / normalizer).astype(jnp.bfloat16).astype(jnp.float32)
    value_copy.wait()
    mixed = jnp.dot(attn_prob, kv[1], preferred_element_type=jnp.float32) + prob_own * new_value
    head_at = lax.broadcasted_iota(jnp.int32, (heads, HEAD_SIZE), 0)
    attended = mixed[:, :HEAD_SIZE]
    for group in range(1, KEY_VALUE_HEADS):
        attended = jnp.where(
            head_at >= group * group_heads,
            mixed[:, group * HEAD_SIZE : (group + 1) * HEAD_SIZE],
            attended,
        )
    levels = (r48[...] + attended).astype(jnp.bfloat16).astype(jnp.float32)
    gain_copy.wait()
    total = jnp.sum(jnp.sum(levels * levels, axis=1, keepdims=True), axis=0, keepdims=True)
    normed = levels * lax.rsqrt(total / (heads * HEAD_SIZE) + 1e-05) * gain[...]
    filler = jnp.zeros((payload.shape[1] - pieces, HEAD_SIZE), jnp.float32)
    for part in range(FSDP):
        payload[part] = jnp.concatenate(
            [normed[part * pieces : (part + 1) * pieces], filler], axis=0
        ).astype(jnp.bfloat16)

    pl.semaphore_wait(barrier, PLANE - 1 + BLOCKS - 1)

    row_copies = []
    for k in range(1, PLANE):
        f2, e2 = plane_peer(k)
        row_copies.append(
            remote(
                payload.at[f2],
                rows_in.at[here],
                row_send_sem.at[k - 1],
                row_recv_sem.at[k - 1],
                (g, f2, e2, t),
            )
        )
        row_copies[-1].start()
    rows_in[here] = payload[f]

    for h in range(heads):
        both_out[0:1, h * HEAD_SIZE : (h + 1) * HEAD_SIZE] = levels[h : h + 1].astype(jnp.bfloat16)

    choices_copy.wait()
    overflow_copy.wait()
    at = lax.broadcasted_iota(jnp.int32, (16, HEAD_SIZE), 0)
    lane = lax.broadcasted_iota(jnp.int32, (16, HEAD_SIZE), 1)
    facts = jnp.zeros((16, HEAD_SIZE), jnp.float32)
    for row in range(16):
        place = row % 4 // 2 * 8 + row // 4 * 2 + row % 2
        for col, value in enumerate((choices[0, row], choices[1, row], overflow[row])):
            facts = jnp.where((at == place) & (lane == col), value.astype(jnp.float32), facts)
    meta[g] = facts
    meta_copy = remote(
        meta.at[g], meta.at[g], pair_send_sem.at[0], pair_recv_sem.at[0], (1 - g, f, e, t)
    )
    meta_copy.start()

    for copy in row_copies:
        copy.wait_recv()
    mine = rows_in[...].astype(jnp.float32)[:, :pieces]
    rows_all[block] = mine.reshape(PLANE * pieces, HEAD_SIZE).astype(jnp.bfloat16)
    block_copies = []
    for k in range(1, BLOCKS):
        _, g2, t2 = block_peer(k)
        block_copies.append(
            remote(
                rows_all.at[block],
                rows_all.at[block],
                block_send_sem.at[k - 1],
                block_recv_sem.at[k - 1],
                (g2, f, e, t2),
            )
        )
        block_copies[-1].start()
    for copy in block_copies:
        copy.wait_recv()

    for b in range(BLOCKS):
        taken = rows_all[b].astype(jnp.float32)
        for i in range(PLANE):
            to = place_of(b * PLANE + i) * pieces
            xs[to : to + pieces, :] = taken[i * pieces : (i + 1) * pieces]
    for j in range(pieces):
        x[:, j * HEAD_SIZE : (j + 1) * HEAD_SIZE] = xs[pl.ds(j, ROWS, stride=pieces), :].astype(
            jnp.bfloat16
        )

    across = (g, 1 - f, e, t)
    def pre_copy(c):
        return remote(
            pre_send.at[c], pre_in.at[c], pre_send_sem.at[c], pre_recv_sem.at[c], across
        )

    def up_step(c, carry):
        up_copy(c).wait()
        partial = lax.dot_general(
            x[...], upw[c], (((1,), (1,)), ((), ())), preferred_element_type=jnp.float32
        )
        pre_mine[c] = partial
        pre_send[c] = partial.astype(jnp.bfloat16)
        pre_copy(c).start()
        return carry

    up_step(0, 0)
    router_copy.wait()
    labels = rt.shape[0]
    logit_mine[...] = jnp.zeros_like(logit_mine)
    logit_mine[:, :labels] = lax.dot_general(
        x[...], rt[...], (((1,), (1,)), ((), ())), preferred_element_type=jnp.float32
    )
    logit_copy = remote(logit_mine, logit_in, pair_send_sem.at[1], pair_recv_sem.at[1], across)
    logit_copy.start()
    lax.fori_loop(1, UP_CHUNKS, up_step, 0)

    meta_copy.wait_recv()
    logit_copy.wait_recv()
    logits = logit_mine[...] + logit_in[...]
    named = jnp.concatenate([meta[0], meta[1]], axis=0)
    label = lax.broadcasted_iota(jnp.int32, logits.shape, 1).astype(jnp.float32)
    first, second, full = named[:, 0:1], named[:, 1:2], named[:, 2:3]
    first_logit = jnp.sum(jnp.where(label == first, logits, 0.0), axis=1, keepdims=True)
    second_logit = jnp.sum(jnp.where(label == second, logits, 0.0), axis=1, keepdims=True)
    first_prob = 1.0 / (1.0 + jnp.exp(second_logit - first_logit))
    kept = first_prob * (1.0 - full)
    my_label = e.astype(jnp.float32)
    gate = jnp.where(first == my_label, kept, 0.0) + jnp.where(second == my_label, 1.0 - kept, 0.0)

    for c in range(UP_CHUNKS):
        down_copy(c).wait()

    def activate(c):
        pre_copy(c).wait_recv()
        value = pre_mine[c] + pre_in[c].astype(jnp.float32)
        act[:, c * hidden : (c + 1) * hidden] = (value / (1.0 + jnp.exp(-value))).astype(
            jnp.bfloat16
        )

    split = (UP_CHUNKS - 1) * hidden
    for c in range(UP_CHUNKS - 1):
        activate(c)
        rows = slice(c * hidden, (c + 1) * hidden)
        product = jnp.dot(act[:, rows], downw[rows, :], preferred_element_type=jnp.float32)
        acc[...] = product if c == 0 else acc[...] + product
    activate(UP_CHUNKS - 1)

    a_copies = [[] for _ in range(OUT_CHUNKS)]
    z_copies = [[] for _ in range(OUT_CHUNKS)]

    def multiply(n):
        cols = slice(n * width, (n + 1) * width)
        value = gate * (
            acc[:, cols]
            + jnp.dot(act[:, split:], downw[split:, cols], preferred_element_type=jnp.float32)
        )
        for b in range(BLOCKS):
            rows = value[b * PLANE : (b + 1) * PLANE]
            folded = jnp.concatenate([rows[:, :half], rows[:, half:]], axis=0)
            own_out[b] = folded
            a_send[n, b] = folded.astype(jnp.bfloat16)
        acc[0:16, n * width : n * width + half] = own_out[block]
        for k in range(1, BLOCKS):
            b2, g2, t2 = block_peer(k)
            at_sem = n * (BLOCKS - 1) + k - 1
            a_copies[n].append(
                remote(
                    a_send.at[n, b2],
                    a_in.at[n, k - 1],
                    a_send_sem.at[at_sem],
                    a_recv_sem.at[at_sem],
                    (g2, f, e, t2),
                )
            )
            a_copies[n][-1].start()

    def add_blocks(n):
        value = acc[0:16, n * width : n * width + half]
        for k in range(1, BLOCKS):
            a_copies[n][k - 1].wait_recv()
            value = value + a_in[n, k - 1].astype(jnp.float32)
        for to in range(EXPERTS):
            for j in range(width // HEAD_SIZE):
                side, col = divmod(j * HEAD_SIZE, half)
                row = side * PLANE + 2 * to
                z_mine[n, to, 2 * j : 2 * j + 2, :] = value[row : row + 2, col : col + HEAD_SIZE]
            z_send[n, to] = z_mine[n, to].astype(jnp.bfloat16)
        for k in range(1, EXPERTS):
            e2 = lax.rem(e + k, EXPERTS)
            at_sem = n * (EXPERTS - 1) + k - 1
            z_copies[n].append(
                remote(
                    z_send.at[n, e2],
                    z_in.at[n, k - 1],
                    z_send_sem.at[at_sem],
                    z_recv_sem.at[at_sem],
                    (g, f, e2, t),
                )
            )
            z_copies[n][-1].start()

    for n in range(OUT_CHUNKS):
        multiply(n)
    for n in range(OUT_CHUNKS):
        add_blocks(n)
    for n in range(OUT_CHUNKS):
        value = z_mine[n, e]
        for k in range(1, EXPERTS):
            z_copies[n][k - 1].wait_recv()
            value = value + z_in[n, k - 1].astype(jnp.float32)
        for j in range(width // HEAD_SIZE):
            at_col = n * width + j * HEAD_SIZE
            for row in range(2):
                to = row * features + at_col
                both_out[1:2, to : to + HEAD_SIZE] = value[2 * j + row : 2 * j + row + 1].astype(
                    jnp.bfloat16
                )

    for copy in row_copies + block_copies + [meta_copy, logit_copy]:
        copy.wait_send()
    for c in range(UP_CHUNKS):
        pre_copy(c).wait_send()
    for n in range(OUT_CHUNKS):
        for copy in a_copies[n] + z_copies[n]:
            copy.wait_send()


def kernel_shards(
    resid,
    query,
    cache,
    new_key_value,
    lengths,
    norm_gain,
    router_weight,
    choices,
    overflow,
    up_weight,
    down_weight,
):
    _, hidden_all, features = up_weight.shape
    hidden = hidden_all // GROUPS
    chunk = hidden // UP_CHUNKS
    width = features // OUT_CHUNKS
    fold = 2 * width // HEAD_SIZE
    pieces = features // HEAD_SIZE
    padded = -(-pieces // 16) * 16
    heads = FSDP * pieces
    kv_features = cache.shape[3]
    f32, bf16 = jnp.float32, jnp.bfloat16
    vmem = pl.BlockSpec(memory_space=pltpu.VMEM)
    hbm = pl.BlockSpec(memory_space=pltpu.HBM)
    dma = pltpu.SemaphoreType.DMA
    both = pl.pallas_call(
        layer_kernel,
        out_shape=jax.ShapeDtypeStruct((2, FSDP * features), bf16),
        in_specs=[hbm] * 11,
        out_specs=vmem,
        scratch_shapes=[
            pltpu.SMEM(lengths.shape, jnp.int32),
            pltpu.SMEM(choices.shape[::-1], jnp.int32),
            pltpu.SMEM(overflow.shape, jnp.int32),
            pltpu.VMEM(resid.shape, bf16),
            pltpu.VMEM(query.shape, bf16),
            pltpu.VMEM((2, kv_features), bf16),
            pltpu.VMEM((heads, HEAD_SIZE), f32),
            pltpu.VMEM((2, CACHE_POSITIONS, kv_features), bf16),
            pltpu.VMEM((router_weight.shape[1], features), bf16),
            pltpu.VMEM((UP_CHUNKS, chunk, features), bf16),
            pltpu.VMEM((hidden, features), bf16),
            pltpu.VMEM((heads, kv_features), f32),
            pltpu.VMEM((heads, HEAD_SIZE), f32),
            pltpu.VMEM((FSDP, padded, HEAD_SIZE), bf16),
            pltpu.VMEM((PLANE, padded, HEAD_SIZE), bf16),
            pltpu.VMEM((BLOCKS, PLANE * pieces, HEAD_SIZE), bf16),
            pltpu.VMEM((ROWS * pieces, HEAD_SIZE), f32),
            pltpu.VMEM((ROWS, features), bf16),
            pltpu.VMEM((GROUPS, 16, HEAD_SIZE), f32),
            pltpu.VMEM((ROWS, HEAD_SIZE), f32),
            pltpu.VMEM((ROWS, HEAD_SIZE), f32),
            pltpu.VMEM((UP_CHUNKS, ROWS, chunk), f32),
            pltpu.VMEM((UP_CHUNKS, ROWS, chunk), bf16),
            pltpu.VMEM((UP_CHUNKS, ROWS, chunk), bf16),
            pltpu.VMEM((ROWS, hidden), bf16),
            pltpu.VMEM((ROWS, features), f32),
            pltpu.VMEM((BLOCKS, 16, width // 2), f32),
            pltpu.VMEM((OUT_CHUNKS, BLOCKS, 16, width // 2), bf16),
            pltpu.VMEM((OUT_CHUNKS, BLOCKS - 1, 16, width // 2), bf16),
            pltpu.VMEM((OUT_CHUNKS, EXPERTS, fold, HEAD_SIZE), f32),
            pltpu.VMEM((OUT_CHUNKS, EXPERTS, fold, HEAD_SIZE), bf16),
            pltpu.VMEM((OUT_CHUNKS, EXPERTS - 1, fold, HEAD_SIZE), bf16),
            dma((10,)),
            dma((UP_CHUNKS,)),
            dma((UP_CHUNKS,)),
            dma((PLANE - 1,)),
            dma((PLANE - 1,)),
            dma((BLOCKS - 1,)),
            dma((BLOCKS - 1,)),
            dma((2,)),
            dma((2,)),
            dma((UP_CHUNKS,)),
            dma((UP_CHUNKS,)),
            dma((OUT_CHUNKS * (BLOCKS - 1),)),
            dma((OUT_CHUNKS * (BLOCKS - 1),)),
            dma((OUT_CHUNKS * (EXPERTS - 1),)),
            dma((OUT_CHUNKS * (EXPERTS - 1),)),
        ],
        compiler_params=pltpu.CompilerParams(
            collective_id=0, has_side_effects=True, vmem_limit_bytes=62 * 1024 * 1024
        ),
        cost_estimate=pl.CostEstimate(
            flops=4 * ROWS * hidden * features,
            bytes_accessed=4 * hidden * features,
            transcendentals=ROWS * hidden,
        ),
        name="layer",
    )(
        lengths,
        choices.T,
        overflow,
        resid,
        query,
        new_key_value.reshape(2, kv_features),
        norm_gain.reshape(heads, HEAD_SIZE),
        cache,
        router_weight.T,
        up_weight,
        down_weight,
    )
    return both[0:1], both[1:2].reshape(2, features)


def solution(mesh):
    sizes = tuple(mesh.shape[name] for name in ("groups", "fsdp", "expert", "tensor"))
    in_kernel = sizes == (GROUPS, FSDP, EXPERTS, CORES)
    return jax.shard_map(
        kernel_shards if in_kernel else shards,
        mesh=mesh,
        in_specs=(
            P(("groups", "fsdp", "expert", "tensor"), None),
            P(("groups", "fsdp", "expert", "tensor"), None),
            P(None, ("groups", "fsdp", "expert", "tensor"), None, None),
            P(None, ("groups", "fsdp", "expert", "tensor"), None),
            P(("groups", "fsdp", "expert", "tensor")),
            P(),
            P(),
            P("groups", None),
            P("groups"),
            P("expert", "tensor", "fsdp"),
            P("expert", "tensor", "fsdp"),
        ),
        out_specs=(
            P(("groups", "fsdp", "expert", "tensor"), None),
            P(("groups", "expert", "tensor"), "fsdp"),
        ),
        check_vma=False,
    )
```
